768 devices in a mesh: ctx: 16 (over x, z_hi), ch: 48 (over z_lo, y, core).
Axes of the slice: x: 4, y: 8, z: 12 (z_hi: 4, z_lo: 3; z = z_hi * 3 + z_lo), core: 2. Of those that a mesh axis runs over, the one named last changes fastest.
Arguments:
- saved_input: float32 [256, 384, 128], P('ctx', 'ch'), may hold values from -6 to 6
- out_grad: float32 [256, 384, 128], P('ctx', 'ch'), may hold values from -0.0068359375 to 0.0068359375
- filter_spec: float32 [2, 16, 256, 256], P(None, None, 'ctx'), as said below
Outputs:
- in_grad: float32 [256, 384, 128], P('ctx', 'ch')
- filter_grad: float32 [256, 16, 128], P('ctx')
The draws below stay inside these ranges and needn't reach their ends.
Inputs may be any that keep to these rules, and one draw needn't show every extreme that they name: `filter_spec`: each filter's spectrum is that of a real sequence of 65536 terms: with k = k1 + 256 * k2, the value at frequency (-k mod 65536) is the complex conjugate of the value at k.
All inputs are finite; a program needn't handle non-finite values.
Results may differ from the reference program's by a relative error of at most 0.0003.
Values sent between devices are 32-bit elements; how exact they have to be, the bound alone decides.
A program may use at most 32 MiB of HBM per device.

```python
import jax
import jax.numpy as jnp
from jax import lax

RADIX = 256
PADDED = 65536
SEQ = 32768
CHANNELS = 384
FILTERS = 16
HEADS = 24


def mirrored(values):
    return jnp.roll(jnp.flip(values, axis=1), 1, axis=1)


def draw_filter_spec(key, part):
    key_real = jax.random.fold_in(key, 11)
    key_imag = jax.random.fold_in(key, 12)
    draw_shape = (FILTERS, RADIX * RADIX)
    spread_scale = (SEQ * HEADS / 2.0) ** 0.5
    first_draw = jax.random.normal(key_real, draw_shape, jnp.float32)
    second_draw = jax.random.normal(key_imag, draw_shape, jnp.float32)
    real_part = (first_draw + mirrored(first_draw)) * spread_scale
    imag_part = (second_draw - mirrored(second_draw)) * spread_scale
    stacked = jnp.stack([real_part, imag_part]).reshape(2, FILTERS, RADIX, RADIX)
    return jnp.transpose(stacked, (0, 1, 3, 2))


def levels(rng, shape, shards, least, largest):
    gain = 1.0
    for position, blocks in shards:
        draws = jax.random.uniform(jax.random.fold_in(jax.random.fold_in(rng, 6), position), (blocks,), jnp.float32, least / len(shards), largest / len(shards))
        gain = gain * jnp.repeat(jnp.exp(draws), shape[position] // blocks).reshape((-1,) + (1,) * (len(shape) - 1 - position))
    return gain


def gaussian(rng, shape, width, limit, cuts=(), kind=jnp.bfloat16):
    values = jax.random.normal(rng, shape, jnp.float32) * width
    if len(cuts) > 0:
        values = levels(rng, shape, cuts, -0.22, 0.18) * values
    return jnp.clip(values, min=-limit, max=limit).astype(kind)


def setup_inputs(seed: int = 0) -> dict:
    splits = jax.random.split(jax.random.key(seed), 4)
    saved_input = gaussian(splits[0], (RADIX, CHANNELS, RADIX // 2), 1.0, 6.0, ((0, 16), (1, 48)), jnp.float32)
    out_grad = gaussian(splits[1], (RADIX, CHANNELS, RADIX // 2), (1.0 / (SEQ * HEADS) ** 0.5), 0.0068359375, ((0, 16), (1, 48)), jnp.float32)
    filter_spec = draw_filter_spec(jax.random.fold_in(splits[3], 71), 0)
    return dict(saved_input=saved_input, out_grad=out_grad, filter_spec=filter_spec)


def reference(saved_input, out_grad, filter_spec):
    spectrum = jnp.transpose(filter_spec, (0, 1, 3, 2)).reshape(2, FILTERS, PADDED)
    spec_real = spectrum[0]
    spec_imag = spectrum[1]
    conj_filter = spec_real - 1j * spec_imag
    pad_count = PADDED - SEQ
    input_seq = jnp.transpose(saved_input, (1, 2, 0)).reshape(CHANNELS, SEQ)
    grad_seq = jnp.transpose(out_grad, (1, 2, 0)).reshape(CHANNELS, SEQ)

    def per_head(totals, head_index):
        row_start = (head_index * FILTERS).astype(jnp.int32)
        inputs = lax.dynamic_slice_in_dim(input_seq, row_start, FILTERS, 0)
        grad_rows = lax.dynamic_slice_in_dim(grad_seq, row_start, FILTERS, 0)
        input_freq = jnp.fft.fft(jnp.pad(inputs, ((0, 0), (0, pad_count))), axis=1)
        grad_freq = jnp.fft.fft(jnp.pad(grad_rows, ((0, 0), (0, pad_count))), axis=1)
        in_grad = jnp.real(jnp.fft.ifft(conj_filter * grad_freq, axis=1))[:, :SEQ]
        product = grad_freq * jnp.conj(input_freq)
        return (totals[0] + jnp.real(product), totals[1] + jnp.imag(product)), in_grad.astype(saved_input.dtype)

    empty_sum = jnp.zeros((FILTERS, PADDED), saved_input.dtype)
    sums, head_grads = lax.scan(per_head, (empty_sum, empty_sum), jnp.arange(HEADS, dtype=jnp.int32))
    head_grads = head_grads.reshape(CHANNELS, RADIX // 2, RADIX)
    in_grad = jnp.transpose(head_grads, (2, 0, 1))
    freq_sum = sums[0] + 1j * sums[1]
    filter_time = jnp.real(jnp.fft.ifft(freq_sum, axis=1))[:, :SEQ].astype(saved_input.dtype)
    filter_grad = jnp.transpose(filter_time.reshape(FILTERS, RADIX // 2, RADIX), (2, 0, 1))
    return in_grad, filter_grad
```

```python
import functools
import math

import jax
import jax.numpy as jnp
import ml_dtypes
import numpy as np
from jax import lax
from jax.experimental import pallas as pl
from jax.experimental.pallas import tpu as pltpu
from jax.sharding import PartitionSpec as P

MESH = pl.DeviceIdType.MESH
RADIX = 256
HALF = 128
PADDED = RADIX * RADIX
NCTX = 16
COLS = 16
CHAN = 8
SLOTS = 8
YS = 8
GROUP = 16
ZS = 3
SPECIAL = 8
F32 = jnp.float32
BF16 = jnp.bfloat16


def split_np(table):
    high = table.astype(np.float32).astype(ml_dtypes.bfloat16)
    low = (table - high.astype(np.float64)).astype(np.float32).astype(ml_dtypes.bfloat16)
    return np.stack([high, low])


def slot_freqs():
    q = np.arange(NCTX)[:, None]
    s = np.arange(SLOTS)[None, :]
    return np.where(q < 8, 16 * q + s, 16 * q + 1 + s)


def angle(product, period):
    return (product % period).astype(np.float64) * (2.0 * math.pi / period)


def tables():
    k1 = slot_freqs()
    a = np.arange(HALF)
    b = np.arange(RADIX)
    alt = 1.0 - 2.0 * (a % 2)
    ang = angle(k1[:, :, None] * a[None, None, :], RADIX)
    first = np.stack([np.cos(ang), -np.sin(ang)], axis=1)
    first[0, 1, 0] = alt
    first = split_np(first.reshape(RADIX, HALF))
    weight = np.full((NCTX, SLOTS, 1), 2.0)
    weight[0, 0] = 1.0
    last = np.stack([weight * np.cos(ang), -weight * np.sin(ang)], axis=1)
    last[0, 1, 0] = alt
    last = split_np(np.ascontiguousarray(last.reshape(RADIX, HALF).T) / PADDED)
    both = angle(b[:, None] * b[None, :], RADIX)
    square = split_np(np.concatenate([np.cos(both), np.sin(both)], axis=1))
    bp = b.reshape(NCTX, COLS)
    lanes = np.tile(bp, (1, CHAN))
    rows = np.concatenate([k1.reshape(-1), np.full(8, HALF)])
    turn = angle(rows[None, :, None] * lanes[:, None, :], PADDED)
    turn = np.stack([np.cos(turn), np.sin(turn)], axis=1).astype(np.float32)
    rows2 = np.concatenate([k1, np.full((NCTX, 8), HALF)], axis=1)
    back = angle(rows2[:, :, None] * b[None, None, :], PADDED)
    back = np.stack([np.cos(back), np.sin(back)], axis=1).astype(np.float32)
    return first, turn, square, back, last


def split(values):
    high = values.astype(BF16)
    low = (values - high.astype(F32)).astype(BF16)
    return high, low


def dot(x, y, dims=((1,), (0,))):
    return lax.dot_general(x, y, (dims, ((), ())), preferred_element_type=F32)


def dot3(x, y, dims=((1,), (0,))):
    return dot(x[0], y[0], dims) + (dot(x[1], y[0], dims) + dot(x[0], y[1], dims))


def block_transpose(parts, lane):
    parts = list(parts)
    for d in (1, 2, 4):
        odd = (lane & (16 * d)) != 0
        fresh = list(parts)
        for j in range(8):
            if j & d == 0:
                lo, hi = parts[j], parts[j + d]
                fresh[j] = jnp.where(odd, pltpu.roll(hi, 16 * d, 1), lo)
                fresh[j + d] = jnp.where(odd, hi, pltpu.roll(lo, 128 - 16 * d, 1))
        parts = fresh
    return parts


def kernel(
    full,
    u_ref, g_ref, h_hbm, first_ref, turn_hbm, square_ref, back_hbm, last_ref,
    in_out, filt_out,
    h_ref, turn_ref, back_ref, send1, recv1, send2, recv2, ext, ext2,
    part, gathered, zpart, everyone,
    local_sem, s1, r1, e1s, e1r, s2, r2, e2s, e2r, rs_s, rs_r, z_s, z_r, ag_s, ag_r,
):
    q = lax.axis_index("ctx")
    ch = lax.axis_index("ch")
    m = ch % GROUP
    zl = ch // GROUP
    core = m % 2
    y = m // 2

    copies = [
        pltpu.make_async_copy(turn_hbm.at[q], turn_ref, local_sem.at[0]),
        pltpu.make_async_copy(h_hbm.at[:, pl.ds(core * CHAN, CHAN)], h_ref, local_sem.at[1]),
        pltpu.make_async_copy(back_hbm.at[q], back_ref, local_sem.at[2]),
    ]
    for copy in copies:
        copy.start()
    recv1[...] = jnp.zeros_like(recv1)
    send1[:, 4] = jnp.zeros((NCTX, 8, HALF), F32)
    ext[...] = jnp.zeros_like(ext)

    barrier = pltpu.get_barrier_semaphore()

    def at_ctx(p):
        return (p, ch)

    def at_group(mm):
        return (q, zl * GROUP + mm)

    def at_z(zz):
        return (q, zz * GROUP + m)

    def greet(device):
        pl.semaphore_signal(barrier, inc=1, device_id=device, device_id_type=MESH)

    def each(count, fn):
        def step(d, carry):
            fn(d)
            return carry

        lax.fori_loop(1, count, step, 0)

    each(NCTX, lambda d: greet(at_ctx((q + d) % NCTX)))
    if full:
        each(GROUP, lambda d: greet(at_group((m + d) % GROUP)))
        each(ZS, lambda d: greet(at_z((zl + d) % ZS)))

    def remote(src, dst, ss, rs, device):
        return pltpu.make_async_remote_copy(
            src_ref=src, dst_ref=dst, send_sem=ss, recv_sem=rs,
            device_id=device, device_id_type=MESH,
        )

    rows = [ref[:, c, :] for ref in (u_ref, g_ref) for c in range(CHAN)]
    x = split(jnp.concatenate(rows, axis=0))
    y1 = dot3((first_ref[0], first_ref[1]), x, ((1,), (1,))).reshape(NCTX, 2, SLOTS, RADIX)
    copies[0].wait()
    sub = lax.broadcasted_iota(jnp.int32, (SLOTS, HALF), 0)
    keep = (lax.broadcasted_iota(jnp.int32, (NCTX, SLOTS, HALF), 0)
            + lax.broadcasted_iota(jnp.int32, (NCTX, SLOTS, HALF), 1)) > 0
    tc = turn_ref[0, :HALF].reshape(NCTX, SLOTS, HALF)
    ts = turn_ref[1, :HALF].reshape(NCTX, SLOTS, HALF)
    ec, es = turn_ref[0, HALF:], turn_ref[1, HALF:]
    extra = jnp.zeros((SLOTS, HALF), F32)
    for f in range(2):
        lanes = slice(f * HALF, (f + 1) * HALF)
        re = y1[:, 0, :, lanes]
        im = y1[:, 1, :, lanes]
        mid = jnp.broadcast_to(im[0, 0:1, :], (SLOTS, HALF))
        extra = jnp.where(sub == 2 * f, mid * ec, extra)
        extra = jnp.where(sub == 2 * f + 1, -mid * es, extra)
        im = jnp.where(keep, im, 0.0)
        send1[:, 2 * f] = re * tc + im * ts
        send1[:, 2 * f + 1] = im * tc - re * ts
    send1[SPECIAL, 4] = extra
    recv1[q] = send1[q]

    peers = NCTX - 1 + ((GROUP - 1 + ZS - 1) if full else 0)
    pl.semaphore_wait(barrier, peers)

    def main1(p):
        return remote(send1.at[p, pl.ds(0, 4)], recv1.at[q, pl.ds(0, 4)], s1.at[p], r1.at[q], at_ctx(p))

    def from1(p):
        return remote(send1.at[p, pl.ds(0, 4)], recv1.at[p, pl.ds(0, 4)], s1.at[p], r1.at[p], at_ctx(p))

    each(NCTX, lambda d: main1((q + d) % NCTX).start())

    ext_send1 = remote(send1.at[SPECIAL, 4], recv1.at[q, 4], e1s.at[0], e1r.at[q], at_ctx(SPECIAL))

    @pl.when(q != SPECIAL)
    def _():
        ext_send1.start()

    copies[1].wait()
    copies[2].wait()
    each(NCTX, lambda d: from1((q + d) % NCTX).wait_recv())

    @pl.when(q == SPECIAL)
    def _():
        each(NCTX, lambda d: remote(
            send1.at[SPECIAL, 4], recv1.at[(q + d) % NCTX, 4], e1s.at[0],
            e1r.at[(q + d) % NCTX], at_ctx((q + d) % NCTX)).wait_recv())

    lane = lax.broadcasted_iota(jnp.int32, (40, HALF), 1)
    halves = [
        block_transpose([recv1[8 * h + j].reshape(40, HALF) for j in range(8)], lane)
        for h in range(2)
    ]
    per_c = [jnp.concatenate([halves[0][c], halves[1][c]], axis=1) for c in range(CHAN)]
    for c in range(CHAN):
        ext[c] = per_c[c][32:40]
    planes = [per_c[c][8 * r : 8 * r + 8] for r in range(4) for c in range(CHAN)]
    planes += [ext[:, r, :] for r in range(4)]
    square = (square_ref[0], square_ref[1])
    spec = dot3(split(jnp.concatenate(planes, axis=0)), square)

    def take(values, r):
        return values[64 * r : 64 * r + 64], values[256 + 8 * r : 256 + 8 * r + 8]

    def forward(values, r):
        out = []
        for re, im in zip(take(values, r), take(values, r + 1)):
            out.append((re[:, :RADIX] + im[:, RADIX:], im[:, :RADIX] - re[:, RADIX:]))
        return out

    us, gs = forward(spec, 0), forward(spec, 2)
    low = q < NCTX // 2
    hr = jnp.where(low, h_ref[0, :, 0:8, :], h_ref[0, :, 1:9, :]).reshape(64, RADIX)
    hi = jnp.where(low, h_ref[1, :, 0:8, :], h_ref[1, :, 1:9, :]).reshape(64, RADIX)
    hs = [(hr, hi), (h_ref[0, :, 0, :], h_ref[1, :, 0, :])]
    groups = []
    for (ar, ai), (gr, gi), (fr, fi) in zip(us, gs, hs):
        groups.append((fr * gr + fi * gi, fr * gi - fi * gr, gr * ar + gi * ai, gi * ar - gr * ai))
    inv = dot3(split(jnp.concatenate(groups[0] + groups[1], axis=0)), square)
    bc, bs = back_ref[0, :8], back_ref[1, :8]
    xc, xs = back_ref[0, 8:], back_ref[1, 8:]
    outs = []
    for f in range(2):
        (re, xr), (im, xi) = take(inv, 2 * f), take(inv, 2 * f + 1)
        qr = (re[:, :RADIX] - im[:, RADIX:]).reshape(CHAN, SLOTS, RADIX)
        qi = (im[:, :RADIX] + re[:, RADIX:]).reshape(CHAN, SLOTS, RADIX)
        outs.append(qr * bc[None] - qi * bs[None])
        outs.append(qi * bc[None] + qr * bs[None])
        er = xr[:, :RADIX] - xi[:, RADIX:]
        ei = xi[:, :RADIX] + xr[:, RADIX:]
        ext2[:, f, :] = er * xc - ei * xs
    for r in range(2, 8):
        ext2[:, r, :] = jnp.zeros((CHAN, RADIX), F32)
    per_c = [jnp.concatenate([o[c] for o in outs] + [ext2[c]], axis=0) for c in range(CHAN)]
    for h in range(2):
        for j, value in enumerate(block_transpose([v[:, h * HALF : (h + 1) * HALF] for v in per_c], lane)):
            send2[8 * h + j] = value.reshape(5, 8, HALF)
    recv2[q, 0:4] = send2[q, 0:4]

    def main2(p):
        return remote(send2.at[p, pl.ds(0, 4)], recv2.at[q, pl.ds(0, 4)], s2.at[p], r2.at[q], at_ctx(p))

    def from2(p):
        return remote(send2.at[p, pl.ds(0, 4)], recv2.at[p, pl.ds(0, 4)], s2.at[p], r2.at[p], at_ctx(p))

    def extra2(p):
        return remote(send2.at[p, 4], recv2.at[SPECIAL, 4], e2s.at[p], e2r.at[0], at_ctx(p))

    @pl.when(q == SPECIAL)
    def _():
        recv2[SPECIAL, 4] = send2[SPECIAL, 4]
        each(NCTX, lambda d: extra2((q + d) % NCTX).start())

    each(NCTX, lambda d: main2((q + d) % NCTX).start())
    each(NCTX, lambda d: from2((q + d) % NCTX).wait_recv())

    @pl.when(q != SPECIAL)
    def _():
        remote(send2.at[0, 4], recv2.at[SPECIAL, 4], e2s.at[0], e2r.at[0], at_ctx(SPECIAL)).wait_recv()

    for f in range(2):
        recv2[0, 2 * f + 1, 0:1, :] = recv2[SPECIAL, 4, f : f + 1, :]
    both = jnp.concatenate(
        [recv2[:, 2 * f : 2 * f + 2].reshape(RADIX, HALF) for f in range(2)], axis=1
    )
    result = dot3((last_ref[0], last_ref[1]), split(both))
    own = result[:, :HALF].T
    for c in range(CHAN):
        in_out[:, c, :] = own[COLS * c : COLS * (c + 1)]
    part[...] = result[:, HALF:].T.reshape(CHAN, COLS, HALF)

    if full:
        def out_rs(yy):
            return remote(part.at[yy], gathered.at[y], rs_s.at[yy], rs_r.at[y], at_group(yy * 2 + core))

        def in_rs(yy):
            return remote(part.at[yy], gathered.at[yy], rs_s.at[yy], rs_r.at[yy], at_group(yy * 2 + core))

        each(YS, lambda d: out_rs((y + d) % YS).start())
        gathered[y] = part[y]
        each(YS, lambda d: in_rs((y + d) % YS).wait_recv())
        zpart[zl] = jnp.sum(gathered[...], axis=0)

        def out_z(zz):
            return remote(zpart.at[zl], zpart.at[zl], z_s.at[zz], z_r.at[zl], at_z(zz))

        def in_z(zz):
            return remote(zpart.at[zz], zpart.at[zz], z_s.at[zz], z_r.at[zz], at_z(zz))

        each(ZS, lambda d: out_z((zl + d) % ZS).start())
        each(ZS, lambda d: in_z((zl + d) % ZS).wait_recv())
        fid = core * CHAN + y
        everyone[fid] = (zpart[0] + zpart[1]) + zpart[2]

        def out_ag(mm):
            return remote(everyone.at[fid], everyone.at[fid], ag_s.at[mm], ag_r.at[m], at_group(mm))

        def in_ag(mm):
            other = (mm % 2) * CHAN + mm // 2
            return remote(everyone.at[other], everyone.at[other], ag_s.at[mm], ag_r.at[mm], at_group(mm))

        each(GROUP, lambda d: out_ag((m + d) % GROUP).start())
        each(GROUP, lambda d: in_ag((m + d) % GROUP).wait_recv())
        for f in range(2 * CHAN):
            filt_out[:, f, :] = everyone[f]
        each(YS, lambda d: out_rs((y + d) % YS).wait_send())
        each(ZS, lambda d: out_z((zl + d) % ZS).wait_send())
        each(GROUP, lambda d: out_ag((m + d) % GROUP).wait_send())
    else:
        for f in range(2 * CHAN):
            filt_out[:, f, :] = part[f % CHAN]

    each(NCTX, lambda d: main1((q + d) % NCTX).wait_send())
    each(NCTX, lambda d: main2((q + d) % NCTX).wait_send())

    @pl.when(q != SPECIAL)
    def _():
        ext_send1.wait_send()

    @pl.when(q == SPECIAL)
    def _():
        each(NCTX, lambda d: extra2((q + d) % NCTX).wait_send())


def body(saved_input, out_grad, filter_spec):
    full = lax.axis_size("ch") > 1
    first, turn, square, back, last = (jnp.asarray(t) for t in tables())
    vm = pl.BlockSpec(memory_space=pltpu.VMEM)
    hbm = pl.BlockSpec(memory_space=pl.ANY)
    sem = pltpu.SemaphoreType.DMA
    v = pltpu.VMEM
    return pl.pallas_call(
        functools.partial(kernel, full),
        out_shape=(
            jax.ShapeDtypeStruct((COLS, CHAN, HALF), F32),
            jax.ShapeDtypeStruct((COLS, 2 * CHAN, HALF), F32),
        ),
        in_specs=[vm, vm, hbm, vm, hbm, vm, hbm, vm],
        out_specs=(vm, vm),
        scratch_shapes=[
            v((2, CHAN, 16, RADIX), F32),
            v((2, HALF + 8, HALF), F32),
            v((2, 16, RADIX), F32),
            v((NCTX, 5, SLOTS, HALF), F32),
            v((NCTX, 5, SLOTS, HALF), F32),
            v((NCTX, 5, SLOTS, HALF), F32),
            v((NCTX, 5, SLOTS, HALF), F32),
            v((CHAN, 8, RADIX), F32),
            v((CHAN, 8, RADIX), F32),
            v((CHAN, COLS, HALF), F32),
            v((YS, COLS, HALF), F32),
            v((ZS, COLS, HALF), F32),
            v((2 * CHAN, COLS, HALF), F32),
            sem((3,)),
            sem((NCTX,)), sem((NCTX,)), sem((1,)), sem((NCTX,)),
            sem((NCTX,)), sem((NCTX,)), sem((NCTX,)), sem((1,)),
            sem((YS,)), sem((YS,)), sem((ZS,)), sem((ZS,)), sem((GROUP,)), sem((GROUP,)),
        ],
        compiler_params=pltpu.CompilerParams(
            collective_id=0, has_side_effects=True, vmem_limit_bytes=24 * 2**20
        ),
        cost_estimate=pl.CostEstimate(flops=400_000_000, bytes_accessed=2_000_000, transcendentals=0),
    )(saved_input, out_grad, filter_spec, first, turn, square, back, last)


def solution(mesh):
    placed = (P("ctx", "ch", None), P("ctx", "ch", None), P(None, None, "ctx", None))
    return jax.shard_map(
        body,
        mesh=mesh,
        in_specs=placed,
        out_specs=(P("ctx", "ch", None), P("ctx", None, None)),
        check_vma=False,
    )
```

```python
import functools
import math

import jax
import jax.numpy as jnp
import ml_dtypes
import numpy as np
from jax import lax
from jax.experimental import pallas as pl
from jax.experimental.pallas import tpu as pltpu
from jax.sharding import PartitionSpec as P

MESH = pl.DeviceIdType.MESH
RADIX = 256
HALF = 128
PADDED = RADIX * RADIX
NCTX = 16
COLS = 16
CHAN = 8
SLOTS = 8
YS = 8
GROUP = 16
ZS = 3
SPECIAL = 8
F32 = jnp.float32
BF16 = jnp.bfloat16


def split_np(table):
    high = table.astype(np.float32).astype(ml_dtypes.bfloat16)
    low = (table - high.astype(np.float64)).astype(np.float32).astype(ml_dtypes.bfloat16)
    return np.stack([high, low])


def slot_freqs():
    q = np.arange(NCTX)[:, None]
    s = np.arange(SLOTS)[None, :]
    return np.where(q < 8, 16 * q + s, 16 * q + 1 + s)


def angle(product, period):
    return (product % period).astype(np.float64) * (2.0 * math.pi / period)


def tables():
    k1 = slot_freqs()
    a = np.arange(HALF)
    b = np.arange(RADIX)
    alt = 1.0 - 2.0 * (a % 2)
    ang = angle(k1[:, :, None] * a[None, None, :], RADIX)
    first = np.stack([np.cos(ang), -np.sin(ang)], axis=1)
    first[0, 1, 0] = alt
    first = split_np(first.reshape(RADIX, HALF))
    weight = np.full((NCTX, SLOTS, 1), 2.0)
    weight[0, 0] = 1.0
    last = np.stack([weight * np.cos(ang), -weight * np.sin(ang)], axis=1)
    last[0, 1, 0] = alt
    last = split_np(np.ascontiguousarray(last.reshape(RADIX, HALF).T) / PADDED)
    both = angle(b[:, None] * b[None, :], RADIX)
    square = split_np(np.concatenate([np.cos(both), np.sin(both)], axis=1))
    bp = b.reshape(NCTX, COLS)
    lanes = np.tile(bp, (1, CHAN))
    rows = np.concatenate([k1.reshape(-1), np.full(8, HALF)])
    turn = angle(rows[None, :, None] * lanes[:, None, :], PADDED)
    turn = np.stack([np.cos(turn), np.sin(turn)], axis=1).astype(np.float32)
    rows2 = np.concatenate([k1, np.full((NCTX, 8), HALF)], axis=1)
    back = angle(rows2[:, :, None] * b[None, None, :], PADDED)
    back = np.stack([np.cos(back), np.sin(back)], axis=1).astype(np.float32)
    return first, turn, square, back, last


def split(values):
    high = values.astype(BF16)
    low = (values - high.astype(F32)).astype(BF16)
    return high, low


def dot(x, y, dims=((1,), (0,))):
    return lax.dot_general(x, y, (dims, ((), ())), preferred_element_type=F32)


def dot3(x, y, dims=((1,), (0,))):
    return dot(x[0], y[0], dims) + (dot(x[1], y[0], dims) + dot(x[0], y[1], dims))


def block_transpose(parts, lane):
    parts = list(parts)
    for d in (1, 2, 4):
        odd = (lane & (16 * d)) != 0
        fresh = list(parts)
        for j in range(8):
            if j & d == 0:
                lo, hi = parts[j], parts[j + d]
                fresh[j] = jnp.where(odd, pltpu.roll(hi, 16 * d, 1), lo)
                fresh[j + d] = jnp.where(odd, hi, pltpu.roll(lo, 128 - 16 * d, 1))
        parts = fresh
    return parts


def kernel(
    full,
    u_ref, g_ref, h_hbm, first_hbm, turn_hbm, square_hbm, back_hbm, last_hbm,
    in_out, filt_out,
    first_ref, square_ref, last_ref,
    h_ref, turn_ref, back_ref, send1, recv1, send2, recv2, ext, ext2,
    part, gathered, zpart, everyone,
    local_sem, s1, r1, s2, r2, rs_s, rs_r, z_s, z_r, ag_s, ag_r, c_s, c_r,
):
    q = lax.axis_index("ctx")
    ch = lax.axis_index("ch")
    m = ch % GROUP
    zl = ch // GROUP
    core = m % 2
    y = m // 2

    copies = [
        pltpu.make_async_copy(first_hbm, first_ref, local_sem.at[0]),
        pltpu.make_async_copy(turn_hbm.at[q], turn_ref, local_sem.at[1]),
        pltpu.make_async_copy(square_hbm, square_ref, local_sem.at[2]),
        pltpu.make_async_copy(h_hbm.at[:, pl.ds(core * CHAN, CHAN)], h_ref, local_sem.at[3]),
        pltpu.make_async_copy(back_hbm.at[q], back_ref, local_sem.at[4]),
        pltpu.make_async_copy(last_hbm, last_ref, local_sem.at[5]),
    ]
    for copy in copies[:2]:
        copy.start()
    recv1[:, 4] = jnp.zeros((NCTX, SLOTS, HALF), F32)

    barrier = pltpu.get_barrier_semaphore()

    def at_ctx(p):
        return (p, ch)

    def at_group(mm):
        return (q, zl * GROUP + mm)

    def at_z(zz):
        return (q, zz * GROUP + m)

    def greet(device):
        pl.semaphore_signal(barrier, inc=1, device_id=device, device_id_type=MESH)

    def each(count, fn):
        def step(d, carry):
            fn(d)
            return carry

        lax.fori_loop(1, count, step, 0)

    each(NCTX, lambda d: greet(at_ctx((q + d) % NCTX)))
    if full:
        each(YS, lambda d: greet(at_group((y + d) % YS * 2 + core)))
        greet(at_group(m + 1 - 2 * core))
        each(ZS, lambda d: greet(at_z((zl + d) % ZS)))
    for copy in copies[2:]:
        copy.start()
    ext2[...] = jnp.zeros_like(ext2)

    def remote(src, dst, ss, rs, device):
        return pltpu.make_async_remote_copy(
            src_ref=src, dst_ref=dst, send_sem=ss, recv_sem=rs,
            device_id=device, device_id_type=MESH,
        )

    copies[0].wait()
    rows = [ref[:, c, :] for ref in (u_ref, g_ref) for c in range(CHAN)]
    x = split(jnp.concatenate(rows, axis=0))
    y1 = dot3((first_ref[0], first_ref[1]), x, ((1,), (1,))).reshape(NCTX, 2, SLOTS, RADIX)
    copies[1].wait()
    sub = lax.broadcasted_iota(jnp.int32, (SLOTS, HALF), 0)
    keep = (lax.broadcasted_iota(jnp.int32, (NCTX, SLOTS, HALF), 0)
            + lax.broadcasted_iota(jnp.int32, (NCTX, SLOTS, HALF), 1)) > 0
    tc = turn_ref[0, :HALF].reshape(NCTX, SLOTS, HALF)
    ts = turn_ref[1, :HALF].reshape(NCTX, SLOTS, HALF)
    ec, es = turn_ref[0, HALF:], turn_ref[1, HALF:]
    extra = jnp.zeros((SLOTS, HALF), F32)
    for f in range(2):
        lanes = slice(f * HALF, (f + 1) * HALF)
        re = y1[:, 0, :, lanes]
        im = y1[:, 1, :, lanes]
        mid = jnp.broadcast_to(im[0, 0:1, :], (SLOTS, HALF))
        extra = jnp.where(sub == 2 * f, mid * ec, extra)
        extra = jnp.where(sub == 2 * f + 1, -mid * es, extra)
        im = jnp.where(keep, im, 0.0)
        send1[:, 2 * f] = re * tc + im * ts
        send1[:, 2 * f + 1] = im * tc - re * ts
    send1[SPECIAL, 4] = extra
    recv1[q, 0:4] = send1[q, 0:4]

    @pl.when(q == SPECIAL)
    def _():
        recv1[SPECIAL, 4] = send1[SPECIAL, 4]

    pl.semaphore_wait(barrier, NCTX - 1 + ((YS - 1 + 1 + ZS - 1) if full else 0))

    def tiles(special, count, act):
        @pl.when(special)
        def _():
            act(count + 1)

        @pl.when(jnp.logical_not(special))
        def _():
            act(count)

    def out1(p, count):
        return remote(
            send1.at[p, pl.ds(0, count)], recv1.at[q, pl.ds(0, count)], s1.at[p], r1.at[q], at_ctx(p))

    def in1(p, count):
        return remote(
            send1.at[p, pl.ds(0, count)], recv1.at[p, pl.ds(0, count)], s1.at[p], r1.at[p], at_ctx(p))

    def start1(d):
        p = (q + d) % NCTX
        tiles(p == SPECIAL, 4, lambda n: out1(p, n).start())

    each(NCTX, start1)
    for copy in copies[2:]:
        copy.wait()
    tiles(q == SPECIAL, 4, lambda n: each(NCTX, lambda d: in1((q + d) % NCTX, n).wait_recv()))

    def lane_ids(rows):
        return lax.broadcasted_iota(jnp.int32, (rows, HALF), 1)

    halves = [
        block_transpose([recv1[8 * h + j].reshape(40, HALF) for j in range(8)], lane_ids(40))
        for h in range(2)
    ]
    per_c = [jnp.concatenate([halves[0][c], halves[1][c]], axis=1) for c in range(CHAN)]
    for c in range(CHAN):
        ext[c] = per_c[c][32:40]
    planes = [per_c[c][8 * r : 8 * r + 8] for r in range(4) for c in range(CHAN)]
    planes += [ext[:, r, :] for r in range(4)]
    square = (square_ref[0], square_ref[1])
    spec = dot3(split(jnp.concatenate(planes, axis=0)), square)

    def forward(r):
        out = []
        for base, size in ((64 * r, 64), (256 + 8 * r, 8)):
            re, im = spec[base : base + size], spec[base + size : base + 2 * size]
            out.append((re[:, :RADIX] + im[:, RADIX:], im[:, :RADIX] - re[:, RADIX:]))
        return out

    us, gs = forward(0), forward(2)
    bc, bs = back_ref[0, :8], back_ref[1, :8]
    xc, xs = back_ref[0, 8:], back_ref[1, 8:]

    def out2(f, p, count):
        return remote(
            send2.at[f, p, pl.ds(0, count)], recv2.at[f, q, pl.ds(0, count)],
            s2.at[f, p], r2.at[f, q], at_ctx(p))

    def in2(f, p, count):
        return remote(
            send2.at[f, p, pl.ds(0, count)], recv2.at[f, p, pl.ds(0, count)],
            s2.at[f, p], r2.at[f, p], at_ctx(p))

    def inverse(f, main, side):
        inv = dot3(split(jnp.concatenate(main + side, axis=0)), square)
        re, im, xr, xi = inv[:64], inv[64:128], inv[128:136], inv[136:144]
        qr = (re[:, :RADIX] - im[:, RADIX:]).reshape(CHAN, SLOTS, RADIX)
        qi = (im[:, :RADIX] + re[:, RADIX:]).reshape(CHAN, SLOTS, RADIX)
        outs = (qr * bc[None] - qi * bs[None], qi * bc[None] + qr * bs[None])
        er = xr[:, :RADIX] - xi[:, RADIX:]
        ei = xi[:, :RADIX] + xr[:, RADIX:]
        ext2[f, :, 0, :] = er * xc - ei * xs
        per_c = [jnp.concatenate([outs[0][c], outs[1][c], ext2[f, c]], axis=0) for c in range(CHAN)]
        for h in range(2):
            parts = [v[:, h * HALF : (h + 1) * HALF] for v in per_c]
            for j, value in enumerate(block_transpose(parts, lane_ids(24))):
                send2[f, 8 * h + j] = value.reshape(3, SLOTS, HALF)
        recv2[f, q] = send2[f, q]
        tiles(q == SPECIAL, 2, lambda n: each(NCTX, lambda d: out2(f, (q + d) % NCTX, n).start()))

    def collect(f):
        def arrive(d):
            p = (q + d) % NCTX
            tiles(p == SPECIAL, 2, lambda n: in2(f, p, n).wait_recv())

        each(NCTX, arrive)
        recv2[f, 0, 1, 0:1, :] = recv2[f, SPECIAL, 2, 0:1, :]
        values = split(recv2[f, :, 0:2].reshape(RADIX, HALF))
        return dot3((last_ref[0], last_ref[1]), values).T

    corr = [
        [gr * ar + gi * ai, gi * ar - gr * ai]
        for (ar, ai), (gr, gi) in zip(us, gs)
    ]
    inverse(0, corr[0], corr[1])
    low = q < NCTX // 2
    hr = jnp.where(low, h_ref[0, :, 0:8, :], h_ref[0, :, 1:9, :]).reshape(64, RADIX)
    hi = jnp.where(low, h_ref[1, :, 0:8, :], h_ref[1, :, 1:9, :]).reshape(64, RADIX)
    hs = [(hr, hi), (h_ref[0, :, 0, :], h_ref[1, :, 0, :])]
    prod = [
        [fr * gr + fi * gi, fr * gi - fi * gr]
        for (fr, fi), (gr, gi) in zip(hs, gs)
    ]
    inverse(1, prod[0], prod[1])

    part[...] = collect(0).reshape(CHAN, COLS, HALF)

    def out_rs(yy):
        return remote(part.at[yy], gathered.at[y], rs_s.at[yy], rs_r.at[y], at_group(yy * 2 + core))

    def in_rs(yy):
        return remote(part.at[yy], gathered.at[yy], rs_s.at[yy], rs_r.at[yy], at_group(yy * 2 + core))

    if full:
        each(YS, lambda d: out_rs((y + d) % YS).start())
        gathered[y] = part[y]

    own = collect(1)
    for c in range(CHAN):
        in_out[:, c, :] = own[COLS * c : COLS * (c + 1)]

    if full:
        each(YS, lambda d: in_rs((y + d) % YS).wait_recv())
        zpart[zl] = jnp.sum(gathered[...], axis=0)

        def out_z(zz):
            return remote(zpart.at[zl], zpart.at[zl], z_s.at[zz], z_r.at[zl], at_z(zz))

        def in_z(zz):
            return remote(zpart.at[zz], zpart.at[zz], z_s.at[zz], z_r.at[zz], at_z(zz))

        each(ZS, lambda d: out_z((zl + d) % ZS).start())
        each(ZS, lambda d: in_z((zl + d) % ZS).wait_recv())
        everyone[core, y] = (zpart[0] + zpart[1]) + zpart[2]
        twin = at_group(m + 1 - 2 * core)

        def out_ag(yy):
            return remote(
                everyone.at[core, y], everyone.at[core, y], ag_s.at[yy], ag_r.at[y], at_group(yy * 2 + core))

        def in_ag(yy):
            return remote(
                everyone.at[core, yy], everyone.at[core, yy], ag_s.at[yy], ag_r.at[yy], at_group(yy * 2 + core))

        def out_twin(yy):
            return remote(everyone.at[core, yy], everyone.at[core, yy], c_s.at[yy], c_r.at[yy], twin)

        def in_twin(yy):
            return remote(everyone.at[1 - core, yy], everyone.at[1 - core, yy], c_s.at[yy], c_r.at[yy], twin)

        def near(d):
            return (y + jnp.where(d % 2 == 1, (d + 1) // 2, YS - d // 2)) % YS

        def hand_on(d):
            in_ag(near(d)).wait_recv()
            out_twin(near(d)).start()

        each(YS, lambda d: out_ag(near(YS - d)).start())
        out_twin(y).start()
        each(YS, hand_on)
        each(YS, lambda d: in_twin(near(d)).wait_recv())
        in_twin(y).wait_recv()
        for f in range(2 * CHAN):
            filt_out[:, f, :] = everyone[f // CHAN, f % CHAN]
        each(YS, lambda d: out_rs((y + d) % YS).wait_send())
        each(ZS, lambda d: out_z((zl + d) % ZS).wait_send())
        each(YS, lambda d: out_ag((y + d) % YS).wait_send())
        each(YS, lambda d: out_twin((y + d) % YS).wait_send())
        out_twin(y).wait_send()
    else:
        for f in range(2 * CHAN):
            filt_out[:, f, :] = part[f % CHAN]

    def finish1(d):
        p = (q + d) % NCTX
        tiles(p == SPECIAL, 4, lambda n: out1(p, n).wait_send())

    each(NCTX, finish1)
    for f in range(2):
        tiles(q == SPECIAL, 2, lambda n: each(NCTX, lambda d: out2(f, (q + d) % NCTX, n).wait_send()))


def body(saved_input, out_grad, filter_spec):
    full = lax.axis_size("ch") > 1
    first, turn, square, back, last = (jnp.asarray(t) for t in tables())
    vm = pl.BlockSpec(memory_space=pltpu.VMEM)
    hbm = pl.BlockSpec(memory_space=pltpu.HBM)
    sem = pltpu.SemaphoreType.DMA
    v = pltpu.VMEM
    return pl.pallas_call(
        functools.partial(kernel, full),
        out_shape=(
            jax.ShapeDtypeStruct((COLS, CHAN, HALF), F32),
            jax.ShapeDtypeStruct((COLS, 2 * CHAN, HALF), F32),
        ),
        in_specs=[vm] * 2 + [hbm] * 6,
        out_specs=(vm, vm),
        scratch_shapes=[
            v((2, RADIX, HALF), BF16),
            v((2, RADIX, 2 * RADIX), BF16),
            v((2, HALF, RADIX), BF16),
            v((2, CHAN, 16, RADIX), F32),
            v((2, HALF + 8, HALF), F32),
            v((2, 16, RADIX), F32),
            v((NCTX, 5, SLOTS, HALF), F32),
            v((NCTX, 5, SLOTS, HALF), F32),
            v((2, NCTX, 3, SLOTS, HALF), F32),
            v((2, NCTX, 3, SLOTS, HALF), F32),
            v((CHAN, 8, RADIX), F32),
            v((2, CHAN, 8, RADIX), F32),
            v((CHAN, COLS, HALF), F32),
            v((YS, COLS, HALF), F32),
            v((ZS, COLS, HALF), F32),
            v((2, CHAN, COLS, HALF), F32),
            sem((6,)),
            sem((NCTX,)), sem((NCTX,)), sem((2, NCTX)), sem((2, NCTX)),
            sem((YS,)), sem((YS,)), sem((ZS,)), sem((ZS,)),
            sem((YS,)), sem((YS,)), sem((YS,)), sem((YS,)),
        ],
        compiler_params=pltpu.CompilerParams(
            collective_id=0, has_side_effects=True, vmem_limit_bytes=56_229_888
        ),
        cost_estimate=pl.CostEstimate(flops=400_000_000, bytes_accessed=2_000_000, transcendentals=0),
    )(saved_input, out_grad, filter_spec, first, turn, square, back, last)


def solution(mesh):
    placed = (P("ctx", "ch", None), P("ctx", "ch", None), P(None, None, "ctx", None))
    return jax.shard_map(
        body,
        mesh=mesh,
        in_specs=placed,
        out_specs=(P("ctx", "ch", None), P("ctx", None, None)),
        check_vma=False,
    )
```

```python
import functools
import math

import jax
import jax.numpy as jnp
import ml_dtypes
import numpy as np
from jax import lax
from jax.experimental import pallas as pl
from jax.experimental.pallas import tpu as pltpu
from jax.sharding import PartitionSpec as P

MESH = pl.DeviceIdType.MESH
RADIX = 256
HALF = 128
PADDED = RADIX * RADIX
NCTX = 16
COLS = 16
CHAN = 8
SLOTS = 8
YS = 8
GROUP = 16
ZS = 3
SPECIAL = 8
F32 = jnp.float32
BF16 = jnp.bfloat16


def split_np(table):
    high = table.astype(np.float32).astype(ml_dtypes.bfloat16)
    low = (table - high.astype(np.float64)).astype(np.float32).astype(ml_dtypes.bfloat16)
    return np.stack([high, low])


def slot_freqs():
    q = np.arange(NCTX)[:, None]
    s = np.arange(SLOTS)[None, :]
    return np.where(q < 8, 16 * q + s, 16 * q + 1 + s)


def angle(product, period):
    return (product % period).astype(np.float64) * (2.0 * math.pi / period)


def tables():
    k1 = slot_freqs()
    a = np.arange(HALF)
    b = np.arange(RADIX)
    alt = 1.0 - 2.0 * (a % 2)
    ang = angle(k1[:, :, None] * a[None, None, :], RADIX)
    first = np.stack([np.cos(ang), -np.sin(ang)], axis=1)
    first[0, 1, 0] = alt
    first = split_np(first.reshape(RADIX, HALF))
    weight = np.full((NCTX, SLOTS, 1), 2.0)
    weight[0, 0] = 1.0
    last = np.stack([weight * np.cos(ang), -weight * np.sin(ang)], axis=1)
    last[0, 1, 0] = alt
    last = split_np(np.ascontiguousarray(last.reshape(RADIX, HALF).T) / PADDED)
    both = angle(b[:, None] * b[None, :], RADIX)
    square = split_np(np.concatenate([np.cos(both), np.sin(both)], axis=1))
    bp = b.reshape(NCTX, COLS)
    lanes = np.tile(bp, (1, CHAN))
    rows = np.concatenate([k1.reshape(-1), np.full(8, HALF)])
    turn = angle(rows[None, :, None] * lanes[:, None, :], PADDED)
    turn = np.stack([np.cos(turn), np.sin(turn)], axis=1).astype(np.float32)
    rows2 = np.concatenate([k1, np.full((NCTX, 8), HALF)], axis=1)
    back = angle(rows2[:, :, None] * b[None, None, :], PADDED)
    back = np.stack([np.cos(back), np.sin(back)], axis=1).astype(np.float32)
    return first, turn, square, back, last


def split(values):
    high = values.astype(BF16)
    low = (values - high.astype(F32)).astype(BF16)
    return high, low


def dot(x, y, dims=((1,), (0,))):
    return lax.dot_general(x, y, (dims, ((), ())), preferred_element_type=F32)


def dot3(x, y, dims=((1,), (0,))):
    return dot(x[0], y[0], dims) + (dot(x[1], y[0], dims) + dot(x[0], y[1], dims))


def block_transpose(parts, lane):
    parts = list(parts)
    for d in (1, 2, 4):
        odd = (lane & (16 * d)) != 0
        fresh = list(parts)
        for j in range(8):
            if j & d == 0:
                lo, hi = parts[j], parts[j + d]
                fresh[j] = jnp.where(odd, pltpu.roll(hi, 16 * d, 1), lo)
                fresh[j + d] = jnp.where(odd, hi, pltpu.roll(lo, 128 - 16 * d, 1))
        parts = fresh
    return parts


def kernel(
    full,
    field_ref, h_hbm, first_hbm, turn_hbm, square_hbm, back_hbm, last_hbm,
    in_out, filt_out,
    first_ref, square_ref, last_ref,
    h_ref, turn_ref, back_ref, send1, recv1, send2, recv2, ext, ext2,
    part, gathered, zpart, everyone,
    local_sem, s1, r1, s2, r2, rs_s, rs_r, z_s, z_r, ag_s, ag_r, c_s, c_r,
):
    q = lax.axis_index("ctx")
    ch = lax.axis_index("ch")
    m = ch % GROUP
    zl = ch // GROUP
    core = m % 2
    y = m // 2

    copies = [
        pltpu.make_async_copy(first_hbm, first_ref, local_sem.at[0]),
        pltpu.make_async_copy(turn_hbm.at[q], turn_ref, local_sem.at[1]),
        pltpu.make_async_copy(square_hbm, square_ref, local_sem.at[2]),
        pltpu.make_async_copy(h_hbm.at[:, pl.ds(core * CHAN, CHAN)], h_ref, local_sem.at[3]),
        pltpu.make_async_copy(back_hbm.at[q], back_ref, local_sem.at[4]),
        pltpu.make_async_copy(last_hbm, last_ref, local_sem.at[5]),
    ]
    for copy in copies[:2]:
        copy.start()
    recv1[:, 4] = jnp.zeros((NCTX, SLOTS, HALF), F32)

    barrier = pltpu.get_barrier_semaphore()

    def at_ctx(p):
        return (p, ch)

    def at_group(mm):
        return (q, zl * GROUP + mm)

    def at_z(zz):
        return (q, zz * GROUP + m)

    def greet(device):
        pl.semaphore_signal(barrier, inc=1, device_id=device, device_id_type=MESH)

    def each(count, fn):
        def step(d, carry):
            fn(d)
            return carry

        lax.fori_loop(1, count, step, 0)

    each(NCTX, lambda d: greet(at_ctx((q + d) % NCTX)))
    if full:
        each(YS, lambda d: greet(at_group((y + d) % YS * 2 + core)))
        greet(at_group(m + 1 - 2 * core))
        each(ZS, lambda d: greet(at_z((zl + d) % ZS)))
    for copy in copies[2:]:
        copy.start()
    ext2[...] = jnp.zeros_like(ext2)

    def remote(src, dst, ss, rs, device):
        return pltpu.make_async_remote_copy(
            src_ref=src, dst_ref=dst, send_sem=ss, recv_sem=rs,
            device_id=device, device_id_type=MESH,
        )

    copies[0].wait()
    rows = [field_ref[f, :, c, :] for f in range(2) for c in range(CHAN)]
    x = split(jnp.concatenate(rows, axis=0))
    y1 = dot3((first_ref[0], first_ref[1]), x, ((1,), (1,))).reshape(NCTX, 2, SLOTS, RADIX)
    copies[1].wait()
    sub = lax.broadcasted_iota(jnp.int32, (SLOTS, HALF), 0)
    keep = (lax.broadcasted_iota(jnp.int32, (NCTX, SLOTS, HALF), 0)
            + lax.broadcasted_iota(jnp.int32, (NCTX, SLOTS, HALF), 1)) > 0
    tc = turn_ref[0, :HALF].reshape(NCTX, SLOTS, HALF)
    ts = turn_ref[1, :HALF].reshape(NCTX, SLOTS, HALF)
    ec, es = turn_ref[0, HALF:], turn_ref[1, HALF:]
    extra = jnp.zeros((SLOTS, HALF), F32)
    for f in range(2):
        lanes = slice(f * HALF, (f + 1) * HALF)
        re = y1[:, 0, :, lanes]
        im = y1[:, 1, :, lanes]
        mid = jnp.broadcast_to(im[0, 0:1, :], (SLOTS, HALF))
        extra = jnp.where(sub == 2 * f, mid * ec, extra)
        extra = jnp.where(sub == 2 * f + 1, -mid * es, extra)
        im = jnp.where(keep, im, 0.0)
        send1[:, 2 * f] = re * tc + im * ts
        send1[:, 2 * f + 1] = im * tc - re * ts
    send1[SPECIAL, 4] = extra
    recv1[q, 0:4] = send1[q, 0:4]

    @pl.when(q == SPECIAL)
    def _():
        recv1[SPECIAL, 4] = send1[SPECIAL, 4]

    pl.semaphore_wait(barrier, NCTX - 1 + ((YS - 1 + 1 + ZS - 1) if full else 0))

    def tiles(special, count, act):
        @pl.when(special)
        def _():
            act(count + 1)

        @pl.when(jnp.logical_not(special))
        def _():
            act(count)

    def out1(p, count):
        return remote(
            send1.at[p, pl.ds(0, count)], recv1.at[q, pl.ds(0, count)], s1.at[p], r1.at[q], at_ctx(p))

    def in1(p, count):
        return remote(
            send1.at[p, pl.ds(0, count)], recv1.at[p, pl.ds(0, count)], s1.at[p], r1.at[p], at_ctx(p))

    def start1(d):
        p = (q + d) % NCTX
        tiles(p == SPECIAL, 4, lambda n: out1(p, n).start())

    each(NCTX, start1)
    for copy in copies[2:]:
        copy.wait()

    def lane_ids(rows):
        return lax.broadcasted_iota(jnp.int32, (rows, HALF), 1)

    square = (square_ref[0], square_ref[1])

    def partial(h):
        def arrive(j):
            p = 8 * h + j

            @pl.when(p != q)
            def _():
                tiles(q == SPECIAL, 4, lambda n: in1(p, n).wait_recv())

        lax.fori_loop(0, 8, lambda j, carry: (arrive(j), carry)[1], 0)
        per_c = block_transpose(
            [recv1[8 * h + j].reshape(40, HALF) for j in range(8)], lane_ids(40))
        for c in range(CHAN):
            ext[c] = per_c[c][32:40]
        planes = [per_c[c][8 * r : 8 * r + 8] for r in range(4) for c in range(CHAN)]
        planes += [ext[:, r, :] for r in range(4)]
        rows = pl.ds(pl.multiple_of(h * HALF, HALF), HALF)
        return dot3(split(jnp.concatenate(planes, axis=0)), (square_ref[0, rows, :], square_ref[1, rows, :]))

    own_half = q // 8
    spec = partial(own_half)
    spec = spec + partial(1 - own_half)

    def forward(r):
        out = []
        for base, size in ((64 * r, 64), (256 + 8 * r, 8)):
            re, im = spec[base : base + size], spec[base + size : base + 2 * size]
            out.append((re[:, :RADIX] + im[:, RADIX:], im[:, :RADIX] - re[:, RADIX:]))
        return out

    us, gs = forward(0), forward(2)
    bc, bs = back_ref[0, :8], back_ref[1, :8]
    xc, xs = back_ref[0, 8:], back_ref[1, 8:]

    def out2(f, p, count):
        return remote(
            send2.at[f, p, pl.ds(0, count)], recv2.at[f, q, pl.ds(0, count)],
            s2.at[f, p], r2.at[f, q], at_ctx(p))

    def in2(f, p, count):
        return remote(
            send2.at[f, p, pl.ds(0, count)], recv2.at[f, p, pl.ds(0, count)],
            s2.at[f, p], r2.at[f, p], at_ctx(p))

    def inverse(f, main, side):
        inv = dot3(split(jnp.concatenate(main + side, axis=0)), square)
        re, im, xr, xi = inv[:64], inv[64:128], inv[128:136], inv[136:144]
        qr = (re[:, :RADIX] - im[:, RADIX:]).reshape(CHAN, SLOTS, RADIX)
        qi = (im[:, :RADIX] + re[:, RADIX:]).reshape(CHAN, SLOTS, RADIX)
        outs = (qr * bc[None] - qi * bs[None], qi * bc[None] + qr * bs[None])
        er = xr[:, :RADIX] - xi[:, RADIX:]
        ei = xi[:, :RADIX] + xr[:, RADIX:]
        ext2[f, :, 0, :] = er * xc - ei * xs
        per_c = [jnp.concatenate([outs[0][c], outs[1][c], ext2[f, c]], axis=0) for c in range(CHAN)]
        for h in range(2):
            parts = [v[:, h * HALF : (h + 1) * HALF] for v in per_c]
            for j, value in enumerate(block_transpose(parts, lane_ids(24))):
                send2[f, 8 * h + j] = value.reshape(3, SLOTS, HALF)
        tiles(q == SPECIAL, 2, lambda n: each(NCTX, lambda d: out2(f, (q + d) % NCTX, n).start()))
        recv2[f, q] = send2[f, q]

    def collect(f):
        def arrive(d):
            p = (q + d) % NCTX
            tiles(p == SPECIAL, 2, lambda n: in2(f, p, n).wait_recv())

        each(NCTX, arrive)
        recv2[f, 0, 1, 0:1, :] = recv2[f, SPECIAL, 2, 0:1, :]
        values = split(recv2[f, :, 0:2].reshape(RADIX, HALF))
        return dot3((last_ref[0], last_ref[1]), values).T

    corr = [
        [gr * ar + gi * ai, gi * ar - gr * ai]
        for (ar, ai), (gr, gi) in zip(us, gs)
    ]
    inverse(0, corr[0], corr[1])
    low = q < NCTX // 2
    hr = jnp.where(low, h_ref[0, :, 0:8, :], h_ref[0, :, 1:9, :]).reshape(64, RADIX)
    hi = jnp.where(low, h_ref[1, :, 0:8, :], h_ref[1, :, 1:9, :]).reshape(64, RADIX)
    hs = [(hr, hi), (h_ref[0, :, 0, :], h_ref[1, :, 0, :])]
    prod = [
        [fr * gr + fi * gi, fr * gi - fi * gr]
        for (fr, fi), (gr, gi) in zip(hs, gs)
    ]
    inverse(1, prod[0], prod[1])

    part[...] = collect(0).reshape(CHAN, COLS, HALF)

    def near(d):
        return (y + jnp.where(d % 2 == 1, (d + 1) // 2, YS - d // 2)) % YS

    def out_rs(yy):
        return remote(part.at[yy], gathered.at[y], rs_s.at[yy], rs_r.at[y], at_group(yy * 2 + core))

    def in_rs(yy):
        return remote(part.at[yy], gathered.at[yy], rs_s.at[yy], rs_r.at[yy], at_group(yy * 2 + core))

    if full:
        each(YS, lambda d: out_rs(near(YS - d)).start())
        gathered[y] = part[y]

    own = collect(1)
    for c in range(CHAN):
        in_out[:, c, :] = own[COLS * c : COLS * (c + 1)]

    if full:
        each(YS, lambda d: in_rs(near(d)).wait_recv())
        zpart[zl] = jnp.sum(gathered[...], axis=0)

        def out_z(zz):
            return remote(zpart.at[zl], zpart.at[zl], z_s.at[zz], z_r.at[zl], at_z(zz))

        def in_z(zz):
            return remote(zpart.at[zz], zpart.at[zz], z_s.at[zz], z_r.at[zz], at_z(zz))

        each(ZS, lambda d: out_z((zl + d) % ZS).start())
        each(ZS, lambda d: in_z((zl + d) % ZS).wait_recv())
        everyone[core, y] = (zpart[0] + zpart[1]) + zpart[2]
        twin = at_group(m + 1 - 2 * core)

        def out_ag(yy):
            return remote(
                everyone.at[core, y], everyone.at[core, y], ag_s.at[yy], ag_r.at[y], at_group(yy * 2 + core))

        def in_ag(yy):
            return remote(
                everyone.at[core, yy], everyone.at[core, yy], ag_s.at[yy], ag_r.at[yy], at_group(yy * 2 + core))

        def out_twin(yy):
            return remote(everyone.at[core, yy], everyone.at[core, yy], c_s.at[yy], c_r.at[yy], twin)

        def in_twin(yy):
            return remote(everyone.at[1 - core, yy], everyone.at[1 - core, yy], c_s.at[yy], c_r.at[yy], twin)

        def hand_on(d):
            in_ag(near(d)).wait_recv()
            out_twin(near(d)).start()

        each(YS, lambda d: out_ag(near(YS - d)).start())
        out_twin(y).start()
        each(YS, hand_on)

        def place(which):
            @pl.when(which == 0)
            def _():
                for f in range(CHAN):
                    filt_out[:, f, :] = everyone[0, f]

            @pl.when(which == 1)
            def _():
                for f in range(CHAN):
                    filt_out[:, CHAN + f, :] = everyone[1, f]

        place(core)
        in_twin(y).wait_recv()
        each(YS, lambda d: in_twin(near(d)).wait_recv())
        place(1 - core)
        each(YS, lambda d: out_rs((y + d) % YS).wait_send())
        each(ZS, lambda d: out_z((zl + d) % ZS).wait_send())
        each(YS, lambda d: out_ag((y + d) % YS).wait_send())
        each(YS, lambda d: out_twin((y + d) % YS).wait_send())
        out_twin(y).wait_send()
    else:
        for f in range(2 * CHAN):
            filt_out[:, f, :] = part[f % CHAN]

    def finish1(d):
        p = (q + d) % NCTX
        tiles(p == SPECIAL, 4, lambda n: out1(p, n).wait_send())

    each(NCTX, finish1)
    for f in range(2):
        tiles(q == SPECIAL, 2, lambda n: each(NCTX, lambda d: out2(f, (q + d) % NCTX, n).wait_send()))


def body(saved_input, out_grad, filter_spec):
    full = lax.axis_size("ch") > 1
    first, turn, square, back, last = (jnp.asarray(t) for t in tables())
    vm = pl.BlockSpec(memory_space=pltpu.VMEM)
    hbm = pl.BlockSpec(memory_space=pltpu.HBM)
    sem = pltpu.SemaphoreType.DMA
    v = pltpu.VMEM
    return pl.pallas_call(
        functools.partial(kernel, full),
        out_shape=(
            jax.ShapeDtypeStruct((COLS, CHAN, HALF), F32),
            jax.ShapeDtypeStruct((COLS, 2 * CHAN, HALF), F32),
        ),
        in_specs=[vm] + [hbm] * 6,
        out_specs=(vm, vm),
        scratch_shapes=[
            v((2, RADIX, HALF), BF16),
            v((2, RADIX, 2 * RADIX), BF16),
            v((2, HALF, RADIX), BF16),
            v((2, CHAN, 16, RADIX), F32),
            v((2, HALF + 8, HALF), F32),
            v((2, 16, RADIX), F32),
            v((NCTX, 5, SLOTS, HALF), F32),
            v((NCTX, 5, SLOTS, HALF), F32),
            v((2, NCTX, 3, SLOTS, HALF), F32),
            v((2, NCTX, 3, SLOTS, HALF), F32),
            v((CHAN, 8, HALF), F32),
            v((2, CHAN, 8, RADIX), F32),
            v((CHAN, COLS, HALF), F32),
            v((YS, COLS, HALF), F32),
            v((ZS, COLS, HALF), F32),
            v((2, CHAN, COLS, HALF), F32),
            sem((6,)),
            sem((NCTX,)), sem((NCTX,)), sem((2, NCTX)), sem((2, NCTX)),
            sem((YS,)), sem((YS,)), sem((ZS,)), sem((ZS,)),
            sem((YS,)), sem((YS,)), sem((YS,)), sem((YS,)),
        ],
        compiler_params=pltpu.CompilerParams(
            collective_id=0, has_side_effects=True, vmem_limit_bytes=56_229_888
        ),
        cost_estimate=pl.CostEstimate(flops=400_000_000, bytes_accessed=2_000_000, transcendentals=0),
    )(jnp.stack([saved_input, out_grad]), filter_spec, first, turn, square, back, last)


def solution(mesh):
    placed = (P("ctx", "ch", None), P("ctx", "ch", None), P(None, None, "ctx", None))
    return jax.shard_map(
        body,
        mesh=mesh,
        in_specs=placed,
        out_specs=(P("ctx", "ch", None), P("ctx", None, None)),
        check_vma=False,
    )
```

```python
import functools
import math

import jax
import jax.numpy as jnp
import ml_dtypes
import numpy as np
from jax import lax
from jax.experimental import pallas as pl
from jax.experimental.pallas import tpu as pltpu
from jax.sharding import PartitionSpec as P

MESH = pl.DeviceIdType.MESH
RADIX = 256
HALF = 128
PADDED = RADIX * RADIX
NCTX = 16
COLS = 16
CHAN = 8
SLOTS = 8
YS = 8
GROUP = 16
ZS = 3
SPECIAL = 8
F32 = jnp.float32
BF16 = jnp.bfloat16


def split_np(table, axis, order):
    high = table.astype(np.float32).astype(ml_dtypes.bfloat16)
    low = (table - high.astype(np.float64)).astype(np.float32).astype(ml_dtypes.bfloat16)
    return np.concatenate([(high, low)[part] for part in order], axis=axis)


def slot_freqs():
    q = np.arange(NCTX)[:, None]
    s = np.arange(SLOTS)[None, :]
    return np.where(q < 8, 16 * q + s, 16 * q + 1 + s)


def angle(product, period):
    return (product % period).astype(np.float64) * (2.0 * math.pi / period)


def tables():
    k1 = slot_freqs()
    a = np.arange(HALF)
    b = np.arange(RADIX)
    alt = 1.0 - 2.0 * (a % 2)
    ang = angle(k1[:, :, None] * a[None, None, :], RADIX)
    first = np.stack([np.cos(ang), -np.sin(ang)], axis=1)
    first[0, 1, 0] = alt
    first = split_np(first.reshape(RADIX, HALF), 1, (0, 1, 0))
    weight = np.full((NCTX, SLOTS, 1), 2.0)
    weight[0, 0] = 1.0
    last = np.stack([weight * np.cos(ang), -weight * np.sin(ang)], axis=1)
    last[0, 1, 0] = alt
    last = split_np(last.reshape(RADIX, HALF).T / PADDED, 1, (0, 1, 0))
    both = angle(b[:, None] * b[None, :], RADIX)
    square = split_np(np.concatenate([np.cos(both), np.sin(both)], axis=1), 0, (0, 0, 1))
    bp = b.reshape(NCTX, COLS)
    lanes = np.tile(bp, (1, CHAN))
    rows = np.concatenate([k1.reshape(-1), np.full(8, HALF)])
    turn = angle(rows[None, :, None] * lanes[:, None, :], PADDED)
    turn = np.stack([np.cos(turn), np.sin(turn)], axis=1).astype(np.float32)
    rows2 = np.concatenate([k1, np.full((NCTX, 8), HALF)], axis=1)
    back = angle(rows2[:, :, None] * b[None, None, :], PADDED)
    back = np.stack([np.cos(back), np.sin(back)], axis=1).astype(np.float32)
    return first, turn, square, back, last


def split(values, axis, order):
    high = values.astype(BF16)
    low = (values - high.astype(F32)).astype(BF16)
    return jnp.concatenate([(high, low)[part] for part in order], axis=axis)


def dot(x, y, dims=((1,), (0,))):
    return lax.dot_general(x, y, (dims, ((), ())), preferred_element_type=F32)


def block_transpose(parts, lane):
    parts = list(parts)
    for d in (1, 2, 4):
        odd = (lane & (16 * d)) != 0
        fresh = list(parts)
        for j in range(8):
            if j & d == 0:
                lo, hi = parts[j], parts[j + d]
                fresh[j] = jnp.where(odd, pltpu.roll(hi, 16 * d, 1), lo)
                fresh[j + d] = jnp.where(odd, hi, pltpu.roll(lo, 128 - 16 * d, 1))
        parts = fresh
    return parts


def kernel(
    full,
    field_ref, h_hbm, first_hbm, turn_hbm, square_hbm, back_hbm, last_hbm,
    in_out, filt_out,
    first_ref, square_ref, last_ref,
    h_ref, turn_ref, back_ref, send1, recv1, send2, recv2, ext, ext2,
    part, gathered, zpart, everyone,
    local_sem, s1, r1, s2, r2, rs_s, rs_r, z_s, z_r, ag_s, ag_r, c_s, c_r,
):
    q = lax.axis_index("ctx")
    ch = lax.axis_index("ch")
    m = ch % GROUP
    zl = ch // GROUP
    core = m % 2
    y = m // 2

    copies = [
        pltpu.make_async_copy(first_hbm, first_ref, local_sem.at[0]),
        pltpu.make_async_copy(turn_hbm.at[q], turn_ref, local_sem.at[1]),
        pltpu.make_async_copy(square_hbm, square_ref, local_sem.at[2]),
        pltpu.make_async_copy(h_hbm.at[:, pl.ds(core * CHAN, CHAN)], h_ref, local_sem.at[3]),
        pltpu.make_async_copy(back_hbm.at[q], back_ref, local_sem.at[4]),
        pltpu.make_async_copy(last_hbm, last_ref, local_sem.at[5]),
    ]
    for copy in copies[:2]:
        copy.start()
    recv1[:, 4] = jnp.zeros((NCTX, SLOTS, HALF), F32)

    barrier = pltpu.get_barrier_semaphore()

    def at_ctx(p):
        return (p, ch)

    def at_group(mm):
        return (q, zl * GROUP + mm)

    def at_z(zz):
        return (q, zz * GROUP + m)

    def greet(device):
        pl.semaphore_signal(barrier, inc=1, device_id=device, device_id_type=MESH)

    def each(count, fn):
        def step(d, carry):
            fn(d)
            return carry

        lax.fori_loop(1, count, step, 0, unroll=True)

    def gray(n):
        return n ^ (n >> 1)

    def far(d):
        return q ^ (4 * gray(3 - ((d - 1) & 3)) + gray(3 - ((d - 1) >> 2)))

    each(NCTX, lambda d: greet(at_ctx(far(d))))
    if full:
        each(YS, lambda d: greet(at_group(((y + d) & (YS - 1)) * 2 + core)))
        greet(at_group(m + 1 - 2 * core))
        each(ZS, lambda d: greet(at_z((zl + d) % ZS)))
    for copy in copies[2:]:
        copy.start()
    ext2[...] = jnp.zeros_like(ext2)

    def remote(src, dst, ss, rs, device):
        return pltpu.make_async_remote_copy(
            src_ref=src, dst_ref=dst, send_sem=ss, recv_sem=rs,
            device_id=device, device_id_type=MESH,
        )

    copies[0].wait()
    rows = [field_ref[f, :, c, :] for f in range(2) for c in range(CHAN)]
    x = split(jnp.concatenate(rows, axis=0), 1, (0, 0, 1))
    y1 = dot(first_ref[...], x, ((1,), (1,))).reshape(NCTX, 2, SLOTS, RADIX)
    copies[1].wait()
    sub = lax.broadcasted_iota(jnp.int32, (SLOTS, HALF), 0)
    keep = (lax.broadcasted_iota(jnp.int32, (NCTX, SLOTS, HALF), 0)
            + lax.broadcasted_iota(jnp.int32, (NCTX, SLOTS, HALF), 1)) > 0
    tc = turn_ref[0, :HALF].reshape(NCTX, SLOTS, HALF)
    ts = turn_ref[1, :HALF].reshape(NCTX, SLOTS, HALF)
    ec, es = turn_ref[0, HALF:], turn_ref[1, HALF:]
    extra = jnp.zeros((SLOTS, HALF), F32)
    for f in range(2):
        lanes = slice(f * HALF, (f + 1) * HALF)
        re = y1[:, 0, :, lanes]
        im = y1[:, 1, :, lanes]
        mid = jnp.broadcast_to(im[0, 0:1, :], (SLOTS, HALF))
        extra = jnp.where(sub == 2 * f, mid * ec, extra)
        extra = jnp.where(sub == 2 * f + 1, -mid * es, extra)
        im = jnp.where(keep, im, 0.0)
        send1[:, 2 * f] = re * tc + im * ts
        send1[:, 2 * f + 1] = im * tc - re * ts
    send1[SPECIAL, 4] = extra
    recv1[q, 0:4] = send1[q, 0:4]

    @pl.when(q == SPECIAL)
    def _():
        recv1[SPECIAL, 4] = send1[SPECIAL, 4]

    pl.semaphore_wait(barrier, NCTX - 1 + ((YS - 1 + 1 + ZS - 1) if full else 0))

    def tiles(special, count, act):
        @pl.when(special)
        def _():
            act(count + 1)

        @pl.when(jnp.logical_not(special))
        def _():
            act(count)

    def out1(p, count):
        return remote(
            send1.at[p, pl.ds(0, count)], recv1.at[q, pl.ds(0, count)], s1.at[p], r1.at[q], at_ctx(p))

    def in1(p, count):
        return remote(
            send1.at[p, pl.ds(0, count)], recv1.at[p, pl.ds(0, count)], s1.at[p], r1.at[p], at_ctx(p))

    def start1(d):
        p = far(d)
        tiles(p == SPECIAL, 4, lambda n: out1(p, n).start())

    each(NCTX, start1)
    for copy in copies[2:]:
        copy.wait()
    tiles(q == SPECIAL, 4, lambda n: each(NCTX, lambda d: in1(((q + d) & (NCTX - 1)), n).wait_recv()))

    def lane_ids(rows):
        return lax.broadcasted_iota(jnp.int32, (rows, HALF), 1)

    halves = [
        block_transpose([recv1[8 * h + j].reshape(40, HALF) for j in range(8)], lane_ids(40))
        for h in range(2)
    ]
    per_c = [jnp.concatenate([halves[0][c], halves[1][c]], axis=1) for c in range(CHAN)]
    for c in range(CHAN):
        ext[c] = per_c[c][32:40]
    planes = [per_c[c][8 * r : 8 * r + 8] for r in range(4) for c in range(CHAN)]
    planes += [ext[:, r, :] for r in range(4)]
    square = square_ref[...]
    spec = dot(split(jnp.concatenate(planes, axis=0), 1, (0, 1, 0)), square)

    def forward(r):
        out = []
        for base, size in ((64 * r, 64), (256 + 8 * r, 8)):
            re, im = spec[base : base + size], spec[base + size : base + 2 * size]
            out.append((re[:, :RADIX] + im[:, RADIX:], im[:, :RADIX] - re[:, RADIX:]))
        return out

    us, gs = forward(0), forward(2)
    bc, bs = back_ref[0, :8], back_ref[1, :8]
    xc, xs = back_ref[0, 8:], back_ref[1, 8:]

    def out2(f, p, count):
        return remote(
            send2.at[f, p, pl.ds(0, count)], recv2.at[f, q, pl.ds(0, count)],
            s2.at[f, p], r2.at[f, q], at_ctx(p))

    def in2(f, p, count):
        return remote(
            send2.at[f, p, pl.ds(0, count)], recv2.at[f, p, pl.ds(0, count)],
            s2.at[f, p], r2.at[f, p], at_ctx(p))

    def inverse(f, main, side):
        inv = dot(split(jnp.concatenate(main + side, axis=0), 1, (0, 1, 0)), square)
        re, im, xr, xi = inv[:64], inv[64:128], inv[128:136], inv[136:144]
        qr = (re[:, :RADIX] - im[:, RADIX:]).reshape(CHAN, SLOTS, RADIX)
        qi = (im[:, :RADIX] + re[:, RADIX:]).reshape(CHAN, SLOTS, RADIX)
        outs = (qr * bc[None] - qi * bs[None], qi * bc[None] + qr * bs[None])
        er = xr[:, :RADIX] - xi[:, RADIX:]
        ei = xi[:, :RADIX] + xr[:, RADIX:]
        ext2[f, :, 0, :] = er * xc - ei * xs
        per_c = [jnp.concatenate([outs[0][c], outs[1][c], ext2[f, c]], axis=0) for c in range(CHAN)]
        for h in range(2):
            parts = [v[:, h * HALF : (h + 1) * HALF] for v in per_c]
            for j, value in enumerate(block_transpose(parts, lane_ids(24))):
                send2[f, 8 * h + j] = value.reshape(3, SLOTS, HALF)
        recv2[f, q] = send2[f, q]

    def leave(f):
        tiles(q == SPECIAL, 2, lambda n: each(NCTX, lambda d: out2(f, far(d), n).start()))


    def collect(f):
        def arrive(d):
            p = ((q + d) & (NCTX - 1))
            tiles(p == SPECIAL, 2, lambda n: in2(f, p, n).wait_recv())

        each(NCTX, arrive)
        recv2[f, 0, 1, 0:1, :] = recv2[f, SPECIAL, 2, 0:1, :]
        values = split(recv2[f, :, 0:2].reshape(RADIX, HALF), 0, (0, 0, 1))
        return dot(last_ref[...], values).T

    corr = [
        [gr * ar + gi * ai, gi * ar - gr * ai]
        for (ar, ai), (gr, gi) in zip(us, gs)
    ]
    inverse(0, corr[0], corr[1])
    leave(0)
    low = q < NCTX // 2
    hr = jnp.where(low, h_ref[0, :, 0:8, :], h_ref[0, :, 1:9, :]).reshape(64, RADIX)
    hi = jnp.where(low, h_ref[1, :, 0:8, :], h_ref[1, :, 1:9, :]).reshape(64, RADIX)
    hs = [(hr, hi), (h_ref[0, :, 0, :], h_ref[1, :, 0, :])]
    prod = [
        [fr * gr + fi * gi, fr * gi - fi * gr]
        for (fr, fi), (gr, gi) in zip(hs, gs)
    ]
    inverse(1, prod[0], prod[1])

    part[...] = collect(0).reshape(CHAN, COLS, HALF)

    def near(d):
        return (y + jnp.where((d & 1) == 1, (d + 1) >> 1, YS - (d >> 1))) & (YS - 1)

    def out_rs(yy):
        return remote(part.at[yy], gathered.at[y], rs_s.at[yy], rs_r.at[y], at_group(yy * 2 + core))

    def in_rs(yy):
        return remote(part.at[yy], gathered.at[yy], rs_s.at[yy], rs_r.at[yy], at_group(yy * 2 + core))

    if full:
        each(YS, lambda d: out_rs(near(YS - d)).start())
        gathered[y] = part[y]

    leave(1)

    if full:
        each(YS, lambda d: in_rs(near(d)).wait_recv())
        zpart[zl] = jnp.sum(gathered[...], axis=0)

        def out_z(zz):
            return remote(zpart.at[zl], zpart.at[zl], z_s.at[zz], z_r.at[zl], at_z(zz))

        def in_z(zz):
            return remote(zpart.at[zz], zpart.at[zz], z_s.at[zz], z_r.at[zz], at_z(zz))

        each(ZS, lambda d: out_z((zl + d) % ZS).start())
        each(ZS, lambda d: in_z((zl + d) % ZS).wait_recv())
        everyone[core, y] = (zpart[0] + zpart[1]) + zpart[2]
        twin = at_group(m + 1 - 2 * core)

        def out_ag(yy):
            return remote(
                everyone.at[core, y], everyone.at[core, y], ag_s.at[yy], ag_r.at[y], at_group(yy * 2 + core))

        def in_ag(yy):
            return remote(
                everyone.at[core, yy], everyone.at[core, yy], ag_s.at[yy], ag_r.at[yy], at_group(yy * 2 + core))

        def out_twin(yy):
            return remote(everyone.at[core, yy], everyone.at[core, yy], c_s.at[yy], c_r.at[yy], twin)

        def in_twin(yy):
            return remote(everyone.at[1 - core, yy], everyone.at[1 - core, yy], c_s.at[yy], c_r.at[yy], twin)

        def hand_on(d):
            in_ag(near(d)).wait_recv()
            out_twin(near(d)).start()

        each(YS, lambda d: out_ag(near(YS - d)).start())
        out_twin(y).start()
        own = collect(1)
        for c in range(CHAN):
            in_out[:, c, :] = own[COLS * c : COLS * (c + 1)]
        each(YS, hand_on)

        def place(which):
            @pl.when(which == 0)
            def _():
                for f in range(CHAN):
                    filt_out[:, f, :] = everyone[0, f]

            @pl.when(which == 1)
            def _():
                for f in range(CHAN):
                    filt_out[:, CHAN + f, :] = everyone[1, f]

        place(core)
        in_twin(y).wait_recv()
        each(YS, lambda d: in_twin(near(d)).wait_recv())
        place(1 - core)
        each(YS, lambda d: out_rs(((y + d) & (YS - 1))).wait_send())
        each(ZS, lambda d: out_z((zl + d) % ZS).wait_send())
        each(YS, lambda d: out_ag(((y + d) & (YS - 1))).wait_send())
        each(YS, lambda d: out_twin(((y + d) & (YS - 1))).wait_send())
        out_twin(y).wait_send()
    else:
        own = collect(1)
        for c in range(CHAN):
            in_out[:, c, :] = own[COLS * c : COLS * (c + 1)]
        for f in range(2 * CHAN):
            filt_out[:, f, :] = part[f % CHAN]

    def finish1(d):
        p = ((q + d) & (NCTX - 1))
        tiles(p == SPECIAL, 4, lambda n: out1(p, n).wait_send())

    each(NCTX, finish1)
    for f in range(2):
        tiles(q == SPECIAL, 2, lambda n: each(NCTX, lambda d: out2(f, ((q + d) & (NCTX - 1)), n).wait_send()))


def body(saved_input, out_grad, filter_spec):
    full = lax.axis_size("ch") > 1
    first, turn, square, back, last = (jnp.asarray(t) for t in tables())
    vm = pl.BlockSpec(memory_space=pltpu.VMEM)
    hbm = pl.BlockSpec(memory_space=pltpu.HBM)
    sem = pltpu.SemaphoreType.DMA
    v = pltpu.VMEM
    return pl.pallas_call(
        functools.partial(kernel, full),
        out_shape=(
            jax.ShapeDtypeStruct((COLS, CHAN, HALF), F32),
            jax.ShapeDtypeStruct((COLS, 2 * CHAN, HALF), F32),
        ),
        in_specs=[vm] + [hbm] * 6,
        out_specs=(vm, vm),
        scratch_shapes=[
            v((RADIX, 3 * HALF), BF16),
            v((3 * RADIX, 2 * RADIX), BF16),
            v((HALF, 3 * RADIX), BF16),
            v((2, CHAN, 16, RADIX), F32),
            v((2, HALF + 8, HALF), F32),
            v((2, 16, RADIX), F32),
            v((NCTX, 5, SLOTS, HALF), F32),
            v((NCTX, 5, SLOTS, HALF), F32),
            v((2, NCTX, 3, SLOTS, HALF), F32),
            v((2, NCTX, 3, SLOTS, HALF), F32),
            v((CHAN, 8, RADIX), F32),
            v((2, CHAN, 8, RADIX), F32),
            v((CHAN, COLS, HALF), F32),
            v((YS, COLS, HALF), F32),
            v((ZS, COLS, HALF), F32),
            v((2, CHAN, COLS, HALF), F32),
            sem((6,)),
            sem((NCTX,)), sem((NCTX,)), sem((2, NCTX)), sem((2, NCTX)),
            sem((YS,)), sem((YS,)), sem((ZS,)), sem((ZS,)),
            sem((YS,)), sem((YS,)), sem((YS,)), sem((YS,)),
        ],
        compiler_params=pltpu.CompilerParams(
            collective_id=0, has_side_effects=True, vmem_limit_bytes=56_229_888
        ),
        cost_estimate=pl.CostEstimate(flops=400_000_000, bytes_accessed=2_000_000, transcendentals=0),
    )(jnp.stack([saved_input, out_grad]), filter_spec, first, turn, square, back, last)


def solution(mesh):
    placed = (P("ctx", "ch", None), P("ctx", "ch", None), P(None, None, "ctx", None))
    return jax.shard_map(
        body,
        mesh=mesh,
        in_specs=placed,
        out_specs=(P("ctx", "ch", None), P("ctx", None, None)),
        check_vma=False,
    )
```

```python
import functools
import math

import jax
import jax.numpy as jnp
import ml_dtypes
import numpy as np
from jax import lax
from jax.experimental import pallas as pl
from jax.experimental.pallas import tpu as pltpu
from jax.sharding import PartitionSpec as P

MESH = pl.DeviceIdType.MESH
RADIX = 256
HALF = 128
PADDED = RADIX * RADIX
NCTX = 16
COLS = 16
CHAN = 8
SLOTS = 8
YS = 8
GROUP = 16
ZS = 3
SPECIAL = 8
F32 = jnp.float32
BF16 = jnp.bfloat16


def split_np(table, axis, order):
    high = table.astype(np.float32).astype(ml_dtypes.bfloat16)
    low = (table - high.astype(np.float64)).astype(np.float32).astype(ml_dtypes.bfloat16)
    return np.concatenate([(high, low)[part] for part in order], axis=axis)


def slot_freqs():
    q = np.arange(NCTX)[:, None]
    s = np.arange(SLOTS)[None, :]
    return np.where(q < 8, 16 * q + s, 16 * q + 1 + s)


def angle(product, period):
    return (product % period).astype(np.float64) * (2.0 * math.pi / period)


def tables():
    k1 = slot_freqs()
    a = np.arange(HALF)
    b = np.arange(RADIX)
    alt = 1.0 - 2.0 * (a % 2)
    ang = angle(k1[:, :, None] * a[None, None, :], RADIX)
    first = np.stack([np.cos(ang), -np.sin(ang)], axis=1)
    first[0, 1, 0] = alt
    first = split_np(first.reshape(RADIX, HALF), 1, (0, 1, 0))
    weight = np.full((NCTX, SLOTS, 1), 2.0)
    weight[0, 0] = 1.0
    last = np.stack([weight * np.cos(ang), -weight * np.sin(ang)], axis=1)
    last[0, 1, 0] = alt
    last = split_np(last.reshape(RADIX, HALF).T / PADDED, 1, (0, 1, 0))
    both = angle(b[:, None] * b[None, :], RADIX)
    square = split_np(np.concatenate([np.cos(both), np.sin(both)], axis=1), 0, (0, 0, 1))
    bp = b.reshape(NCTX, COLS)
    lanes = np.tile(bp, (1, CHAN))
    rows = np.concatenate([k1.reshape(-1), np.full(8, HALF)])
    turn = angle(rows[None, :, None] * lanes[:, None, :], PADDED)
    turn = np.stack([np.cos(turn), np.sin(turn)], axis=1).astype(np.float32)
    rows2 = np.concatenate([k1, np.full((NCTX, 8), HALF)], axis=1)
    back = angle(rows2[:, :, None] * b[None, None, :], PADDED)
    back = np.stack([np.cos(back), np.sin(back)], axis=1).astype(np.float32)
    return first, turn, square, back, last


def split(values, axis, order):
    high = values.astype(BF16)
    low = (values - high.astype(F32)).astype(BF16)
    return jnp.concatenate([(high, low)[part] for part in order], axis=axis)


def dot(x, y, dims=((1,), (0,))):
    return lax.dot_general(x, y, (dims, ((), ())), preferred_element_type=F32)


def block_transpose(parts, lane):
    parts = list(parts)
    for d in (1, 2, 4):
        odd = (lane & (16 * d)) != 0
        fresh = list(parts)
        for j in range(8):
            if j & d == 0:
                lo, hi = parts[j], parts[j + d]
                fresh[j] = jnp.where(odd, pltpu.roll(hi, 16 * d, 1), lo)
                fresh[j + d] = jnp.where(odd, hi, pltpu.roll(lo, 128 - 16 * d, 1))
        parts = fresh
    return parts


def kernel(
    full,
    field_ref, h_hbm, first_hbm, turn_hbm, square_hbm, back_hbm, last_hbm,
    in_out, filt_out,
    first_ref, square_ref, last_ref,
    h_ref, turn_ref, back_ref, send1, recv1, send2, recv2, ext, ext2,
    part, gathered, zpart, everyone,
    local_sem, s1, r1, s2, r2, rs_s, rs_r, z_s, z_r, ag_s, ag_r, c_s, c_r,
):
    q = lax.axis_index("ctx")
    ch = lax.axis_index("ch")
    m = ch % GROUP
    zl = ch // GROUP
    core = m % 2
    y = m // 2

    copies = [
        pltpu.make_async_copy(first_hbm, first_ref, local_sem.at[0]),
        pltpu.make_async_copy(turn_hbm.at[q], turn_ref, local_sem.at[1]),
        pltpu.make_async_copy(square_hbm, square_ref, local_sem.at[2]),
        pltpu.make_async_copy(h_hbm.at[:, pl.ds(core * CHAN, CHAN)], h_ref, local_sem.at[3]),
        pltpu.make_async_copy(back_hbm.at[q], back_ref, local_sem.at[4]),
        pltpu.make_async_copy(last_hbm, last_ref, local_sem.at[5]),
    ]
    for copy in copies[:2]:
        copy.start()
    recv1[:, 4] = jnp.zeros((NCTX, SLOTS, HALF), F32)

    barrier = pltpu.get_barrier_semaphore()

    def at_ctx(p):
        return (p, ch)

    def at_group(mm):
        return (q, zl * GROUP + mm)

    def at_z(zz):
        return (q, zz * GROUP + m)

    def greet(device):
        pl.semaphore_signal(barrier, inc=1, device_id=device, device_id_type=MESH)

    def each(count, fn):
        def step(d, carry):
            fn(d)
            return carry

        lax.fori_loop(1, count, step, 0, unroll=True)

    def gray(n):
        return n ^ (n >> 1)

    def far(d):
        i = d - 1
        mixed = (i >= 4) & (i < 12)
        xi = jnp.where(mixed, (i - 4) >> 1, i & 3)
        zz = jnp.where(mixed, 3 - 2 * (i & 1), jnp.where(i < 4, 2, 0))
        return q ^ (4 * gray(3 - xi) + zz)

    each(NCTX, lambda d: greet(at_ctx(far(d))))
    if full:
        each(YS, lambda d: greet(at_group(((y + d) & (YS - 1)) * 2 + core)))
        greet(at_group(m + 1 - 2 * core))
        each(ZS, lambda d: greet(at_z((zl + d) % ZS)))
    for copy in copies[2:]:
        copy.start()
    ext2[...] = jnp.zeros_like(ext2)

    def remote(src, dst, ss, rs, device):
        return pltpu.make_async_remote_copy(
            src_ref=src, dst_ref=dst, send_sem=ss, recv_sem=rs,
            device_id=device, device_id_type=MESH,
        )

    copies[0].wait()
    rows = [field_ref[f, :, c, :] for f in range(2) for c in range(CHAN)]
    x = split(jnp.concatenate(rows, axis=0), 1, (0, 0, 1))
    y1 = dot(first_ref[...], x, ((1,), (1,))).reshape(NCTX, 2, SLOTS, RADIX)
    copies[1].wait()
    sub = lax.broadcasted_iota(jnp.int32, (SLOTS, HALF), 0)
    keep = (lax.broadcasted_iota(jnp.int32, (NCTX, SLOTS, HALF), 0)
            + lax.broadcasted_iota(jnp.int32, (NCTX, SLOTS, HALF), 1)) > 0
    tc = turn_ref[0, :HALF].reshape(NCTX, SLOTS, HALF)
    ts = turn_ref[1, :HALF].reshape(NCTX, SLOTS, HALF)
    ec, es = turn_ref[0, HALF:], turn_ref[1, HALF:]
    extra = jnp.zeros((SLOTS, HALF), F32)
    for f in range(2):
        lanes = slice(f * HALF, (f + 1) * HALF)
        re = y1[:, 0, :, lanes]
        im = y1[:, 1, :, lanes]
        mid = jnp.broadcast_to(im[0, 0:1, :], (SLOTS, HALF))
        extra = jnp.where(sub == 2 * f, mid * ec, extra)
        extra = jnp.where(sub == 2 * f + 1, -mid * es, extra)
        im = jnp.where(keep, im, 0.0)
        send1[:, 2 * f] = re * tc + im * ts
        send1[:, 2 * f + 1] = im * tc - re * ts
    send1[SPECIAL, 4] = extra
    recv1[q, 0:4] = send1[q, 0:4]

    @pl.when(q == SPECIAL)
    def _():
        recv1[SPECIAL, 4] = send1[SPECIAL, 4]

    pl.semaphore_wait(barrier, NCTX - 1 + ((YS - 1 + 1 + ZS - 1) if full else 0))

    def tiles(special, count, act):
        @pl.when(special)
        def _():
            act(count + 1)

        @pl.when(jnp.logical_not(special))
        def _():
            act(count)

    def out1(p, count):
        return remote(
            send1.at[p, pl.ds(0, count)], recv1.at[q, pl.ds(0, count)], s1.at[p], r1.at[q], at_ctx(p))

    def in1(p, count):
        return remote(
            send1.at[p, pl.ds(0, count)], recv1.at[p, pl.ds(0, count)], s1.at[p], r1.at[p], at_ctx(p))

    def start1(d):
        p = far(d)
        tiles(p == SPECIAL, 4, lambda n: out1(p, n).start())

    each(NCTX, start1)
    for copy in copies[2:]:
        copy.wait()
    tiles(q == SPECIAL, 4, lambda n: each(NCTX, lambda d: in1(((q + d) & (NCTX - 1)), n).wait_recv()))

    def lane_ids(rows):
        return lax.broadcasted_iota(jnp.int32, (rows, HALF), 1)

    halves = [
        block_transpose([recv1[8 * h + j].reshape(40, HALF) for j in range(8)], lane_ids(40))
        for h in range(2)
    ]
    per_c = [jnp.concatenate([halves[0][c], halves[1][c]], axis=1) for c in range(CHAN)]
    for c in range(CHAN):
        ext[c] = per_c[c][32:40]
    planes = [per_c[c][8 * r : 8 * r + 8] for r in range(4) for c in range(CHAN)]
    planes += [ext[:, r, :] for r in range(4)]
    square = square_ref[...]
    spec = dot(split(jnp.concatenate(planes, axis=0), 1, (0, 1, 0)), square)

    def forward(r):
        out = []
        for base, size in ((64 * r, 64), (256 + 8 * r, 8)):
            re, im = spec[base : base + size], spec[base + size : base + 2 * size]
            out.append((re[:, :RADIX] + im[:, RADIX:], im[:, :RADIX] - re[:, RADIX:]))
        return out

    us, gs = forward(0), forward(2)
    bc, bs = back_ref[0, :8], back_ref[1, :8]
    xc, xs = back_ref[0, 8:], back_ref[1, 8:]

    def out2(f, p, count):
        return remote(
            send2.at[f, p, pl.ds(0, count)], recv2.at[f, q, pl.ds(0, count)],
            s2.at[f, p], r2.at[f, q], at_ctx(p))

    def in2(f, p, count):
        return remote(
            send2.at[f, p, pl.ds(0, count)], recv2.at[f, p, pl.ds(0, count)],
            s2.at[f, p], r2.at[f, p], at_ctx(p))

    def inverse(f, main, side):
        inv = dot(split(jnp.concatenate(main + side, axis=0), 1, (0, 1, 0)), square)
        re, im, xr, xi = inv[:64], inv[64:128], inv[128:136], inv[136:144]
        qr = (re[:, :RADIX] - im[:, RADIX:]).reshape(CHAN, SLOTS, RADIX)
        qi = (im[:, :RADIX] + re[:, RADIX:]).reshape(CHAN, SLOTS, RADIX)
        outs = (qr * bc[None] - qi * bs[None], qi * bc[None] + qr * bs[None])
        er = xr[:, :RADIX] - xi[:, RADIX:]
        ei = xi[:, :RADIX] + xr[:, RADIX:]
        ext2[f, :, 0, :] = er * xc - ei * xs
        per_c = [jnp.concatenate([outs[0][c], outs[1][c], ext2[f, c]], axis=0) for c in range(CHAN)]
        for h in range(2):
            parts = [v[:, h * HALF : (h + 1) * HALF] for v in per_c]
            for j, value in enumerate(block_transpose(parts, lane_ids(24))):
                send2[f, 8 * h + j] = value.reshape(3, SLOTS, HALF)
        recv2[f, q] = send2[f, q]

    def leave(f):
        tiles(q == SPECIAL, 2, lambda n: each(NCTX, lambda d: out2(f, far(d), n).start()))


    def collect(f):
        def arrive(d):
            p = ((q + d) & (NCTX - 1))
            tiles(p == SPECIAL, 2, lambda n: in2(f, p, n).wait_recv())

        each(NCTX, arrive)
        recv2[f, 0, 1, 0:1, :] = recv2[f, SPECIAL, 2, 0:1, :]
        values = split(recv2[f, :, 0:2].reshape(RADIX, HALF), 0, (0, 0, 1))
        return dot(last_ref[...], values).T

    corr = [
        [gr * ar + gi * ai, gi * ar - gr * ai]
        for (ar, ai), (gr, gi) in zip(us, gs)
    ]
    inverse(0, corr[0], corr[1])
    leave(0)
    low = q < NCTX // 2
    hr = jnp.where(low, h_ref[0, :, 0:8, :], h_ref[0, :, 1:9, :]).reshape(64, RADIX)
    hi = jnp.where(low, h_ref[1, :, 0:8, :], h_ref[1, :, 1:9, :]).reshape(64, RADIX)
    hs = [(hr, hi), (h_ref[0, :, 0, :], h_ref[1, :, 0, :])]
    prod = [
        [fr * gr + fi * gi, fr * gi - fi * gr]
        for (fr, fi), (gr, gi) in zip(hs, gs)
    ]
    inverse(1, prod[0], prod[1])

    part[...] = collect(0).reshape(CHAN, COLS, HALF)

    def near(d):
        return (y + jnp.where((d & 1) == 1, (d + 1) >> 1, YS - (d >> 1))) & (YS - 1)

    def out_rs(yy):
        return remote(part.at[yy], gathered.at[y], rs_s.at[yy], rs_r.at[y], at_group(yy * 2 + core))

    def in_rs(yy):
        return remote(part.at[yy], gathered.at[yy], rs_s.at[yy], rs_r.at[yy], at_group(yy * 2 + core))

    if full:
        each(YS, lambda d: out_rs(near(YS - d)).start())
        gathered[y] = part[y]

    leave(1)

    if full:
        each(YS, lambda d: in_rs(near(d)).wait_recv())
        zpart[zl] = jnp.sum(gathered[...], axis=0)

        def out_z(zz):
            return remote(zpart.at[zl], zpart.at[zl], z_s.at[zz], z_r.at[zl], at_z(zz))

        def in_z(zz):
            return remote(zpart.at[zz], zpart.at[zz], z_s.at[zz], z_r.at[zz], at_z(zz))

        each(ZS, lambda d: out_z((zl + d) % ZS).start())
        each(ZS, lambda d: in_z((zl + d) % ZS).wait_recv())
        everyone[core, y] = (zpart[0] + zpart[1]) + zpart[2]
        twin = at_group(m + 1 - 2 * core)

        def out_ag(yy):
            return remote(
                everyone.at[core, y], everyone.at[core, y], ag_s.at[yy], ag_r.at[y], at_group(yy * 2 + core))

        def in_ag(yy):
            return remote(
                everyone.at[core, yy], everyone.at[core, yy], ag_s.at[yy], ag_r.at[yy], at_group(yy * 2 + core))

        def out_twin(yy):
            return remote(everyone.at[core, yy], everyone.at[core, yy], c_s.at[yy], c_r.at[yy], twin)

        def in_twin(yy):
            return remote(everyone.at[1 - core, yy], everyone.at[1 - core, yy], c_s.at[yy], c_r.at[yy], twin)

        def hand_on(d):
            in_ag(near(d)).wait_recv()
            out_twin(near(d)).start()

        each(YS, lambda d: out_ag(near(YS - d)).start())
        out_twin(y).start()
        own = collect(1)
        for c in range(CHAN):
            in_out[:, c, :] = own[COLS * c : COLS * (c + 1)]
        each(YS, hand_on)

        def place(which):
            @pl.when(which == 0)
            def _():
                for f in range(CHAN):
                    filt_out[:, f, :] = everyone[0, f]

            @pl.when(which == 1)
            def _():
                for f in range(CHAN):
                    filt_out[:, CHAN + f, :] = everyone[1, f]

        place(core)
        in_twin(y).wait_recv()
        each(YS, lambda d: in_twin(near(d)).wait_recv())
        place(1 - core)
        each(YS, lambda d: out_rs(((y + d) & (YS - 1))).wait_send())
        each(ZS, lambda d: out_z((zl + d) % ZS).wait_send())
        each(YS, lambda d: out_ag(((y + d) & (YS - 1))).wait_send())
        each(YS, lambda d: out_twin(((y + d) & (YS - 1))).wait_send())
        out_twin(y).wait_send()
    else:
        own = collect(1)
        for c in range(CHAN):
            in_out[:, c, :] = own[COLS * c : COLS * (c + 1)]
        for f in range(2 * CHAN):
            filt_out[:, f, :] = part[f % CHAN]

    def finish1(d):
        p = ((q + d) & (NCTX - 1))
        tiles(p == SPECIAL, 4, lambda n: out1(p, n).wait_send())

    each(NCTX, finish1)
    for f in range(2):
        tiles(q == SPECIAL, 2, lambda n: each(NCTX, lambda d: out2(f, ((q + d) & (NCTX - 1)), n).wait_send()))


def body(saved_input, out_grad, filter_spec):
    full = lax.axis_size("ch") > 1
    first, turn, square, back, last = (jnp.asarray(t) for t in tables())
    vm = pl.BlockSpec(memory_space=pltpu.VMEM)
    hbm = pl.BlockSpec(memory_space=pltpu.HBM)
    sem = pltpu.SemaphoreType.DMA
    v = pltpu.VMEM
    return pl.pallas_call(
        functools.partial(kernel, full),
        out_shape=(
            jax.ShapeDtypeStruct((COLS, CHAN, HALF), F32),
            jax.ShapeDtypeStruct((COLS, 2 * CHAN, HALF), F32),
        ),
        in_specs=[vm] + [hbm] * 6,
        out_specs=(vm, vm),
        scratch_shapes=[
            v((RADIX, 3 * HALF), BF16),
            v((3 * RADIX, 2 * RADIX), BF16),
            v((HALF, 3 * RADIX), BF16),
            v((2, CHAN, 16, RADIX), F32),
            v((2, HALF + 8, HALF), F32),
            v((2, 16, RADIX), F32),
            v((NCTX, 5, SLOTS, HALF), F32),
            v((NCTX, 5, SLOTS, HALF), F32),
            v((2, NCTX, 3, SLOTS, HALF), F32),
            v((2, NCTX, 3, SLOTS, HALF), F32),
            v((CHAN, 8, RADIX), F32),
            v((2, CHAN, 8, RADIX), F32),
            v((CHAN, COLS, HALF), F32),
            v((YS, COLS, HALF), F32),
            v((ZS, COLS, HALF), F32),
            v((2, CHAN, COLS, HALF), F32),
            sem((6,)),
            sem((NCTX,)), sem((NCTX,)), sem((2, NCTX)), sem((2, NCTX)),
            sem((YS,)), sem((YS,)), sem((ZS,)), sem((ZS,)),
            sem((YS,)), sem((YS,)), sem((YS,)), sem((YS,)),
        ],
        compiler_params=pltpu.CompilerParams(
            collective_id=0, has_side_effects=True, vmem_limit_bytes=56_229_888
        ),
        cost_estimate=pl.CostEstimate(flops=400_000_000, bytes_accessed=2_000_000, transcendentals=0),
    )(jnp.stack([saved_input, out_grad]), filter_spec, first, turn, square, back, last)


def solution(mesh):
    placed = (P("ctx", "ch", None), P("ctx", "ch", None), P(None, None, "ctx", None))
    return jax.shard_map(
        body,
        mesh=mesh,
        in_specs=placed,
        out_specs=(P("ctx", "ch", None), P("ctx", None, None)),
        check_vma=False,
    )
```

```python
import functools
import math

import jax
import jax.numpy as jnp
import ml_dtypes
import numpy as np
from jax import lax
from jax.experimental import pallas as pl
from jax.experimental.pallas import tpu as pltpu
from jax.sharding import PartitionSpec as P

MESH = pl.DeviceIdType.MESH
RADIX = 256
HALF = 128
PADDED = RADIX * RADIX
NCTX = 16
COLS = 16
CHAN = 8
SLOTS = 8
YS = 8
GROUP = 16
ZS = 3
TRIPLE = 24
SPECIAL = 8
F32 = jnp.float32
BF16 = jnp.bfloat16


def split_np(table, axis, order):
    high = table.astype(np.float32).astype(ml_dtypes.bfloat16)
    low = (table - high.astype(np.float64)).astype(np.float32).astype(ml_dtypes.bfloat16)
    return np.concatenate([(high, low)[part] for part in order], axis=axis)


def slot_freqs():
    q = np.arange(NCTX)[:, None]
    s = np.arange(SLOTS)[None, :]
    return np.where(q < 8, 16 * q + s, 16 * q + 1 + s)


def angle(product, period):
    return (product % period).astype(np.float64) * (2.0 * math.pi / period)


def tables():
    k1 = slot_freqs()
    a = np.arange(HALF)
    b = np.arange(RADIX)
    alt = 1.0 - 2.0 * (a % 2)
    ang = angle(k1[:, :, None] * a[None, None, :], RADIX)
    first = np.stack([np.cos(ang), -np.sin(ang)], axis=1)
    first[0, 1, 0] = alt
    first = split_np(first.reshape(RADIX, HALF), 1, (0, 1, 0))
    weight = np.full((NCTX, SLOTS, 1), 2.0)
    weight[0, 0] = 1.0
    last = np.stack([weight * np.cos(ang), -weight * np.sin(ang)], axis=1)
    last[0, 1, 0] = alt
    last = split_np(last.reshape(RADIX, HALF).T / PADDED, 1, (0, 1, 0))
    both = angle(b[:, None] * b[None, :], RADIX)
    square = split_np(np.concatenate([np.cos(both), np.sin(both)], axis=1), 0, (0, 0, 1))
    bp = b.reshape(NCTX, COLS)
    lanes = np.tile(bp, (1, CHAN))
    rows = np.concatenate([k1.reshape(-1), np.full(8, HALF)])
    turn = angle(rows[None, :, None] * lanes[:, None, :], PADDED)
    turn = np.stack([np.cos(turn), np.sin(turn)], axis=1).astype(np.float32)
    rows2 = np.concatenate([k1, np.full((NCTX, 8), HALF)], axis=1)
    back = angle(rows2[:, :, None] * b[None, None, :], PADDED)
    back = np.stack([np.cos(back), np.sin(back)], axis=1).astype(np.float32)
    return first, turn, square, back, last


def split(values, axis, order):
    high = values.astype(BF16)
    low = (values - high.astype(F32)).astype(BF16)
    return jnp.concatenate([(high, low)[part] for part in order], axis=axis)


def dot(x, y, dims=((1,), (0,))):
    return lax.dot_general(x, y, (dims, ((), ())), preferred_element_type=F32)


def block_transpose(parts, lane):
    parts = list(parts)
    for d in (1, 2, 4):
        odd = (lane & (16 * d)) != 0
        fresh = list(parts)
        for j in range(8):
            if j & d == 0:
                lo, hi = parts[j], parts[j + d]
                fresh[j] = jnp.where(odd, pltpu.roll(hi, 16 * d, 1), lo)
                fresh[j + d] = jnp.where(odd, hi, pltpu.roll(lo, 128 - 16 * d, 1))
        parts = fresh
    return parts


def kernel(
    full,
    field_ref, h_hbm, first_hbm, turn_hbm, square_hbm, back_hbm, last_hbm,
    in_out, filt_out,
    first_ref, square_ref, last_ref,
    h_ref, turn_ref, back_ref, send1, recv1, send2, recv2, ext, ext2,
    part, gathered, everyone,
    local_sem, s1, r1, s2, r2, rs_s, rs_r, ag_s, ag_r, c_s, c_r,
):
    q = lax.axis_index("ctx")
    ch = lax.axis_index("ch")
    m = ch % GROUP
    zl = ch // GROUP
    core = m % 2
    y = m // 2

    copies = [
        pltpu.make_async_copy(first_hbm, first_ref, local_sem.at[0]),
        pltpu.make_async_copy(turn_hbm.at[q], turn_ref, local_sem.at[1]),
        pltpu.make_async_copy(square_hbm, square_ref, local_sem.at[2]),
        pltpu.make_async_copy(h_hbm.at[:, pl.ds(core * CHAN, CHAN)], h_ref, local_sem.at[3]),
        pltpu.make_async_copy(back_hbm.at[q], back_ref, local_sem.at[4]),
        pltpu.make_async_copy(last_hbm, last_ref, local_sem.at[5]),
    ]
    for copy in copies[:2]:
        copy.start()
    recv1[:, 4] = jnp.zeros((NCTX, SLOTS, HALF), F32)

    barrier = pltpu.get_barrier_semaphore()

    def at_ctx(p):
        return (p, ch)

    def at_group(mm):
        return (q, zl * GROUP + mm)

    me = zl * YS + y

    def at_triple(t):
        return (q, (t // YS) * GROUP + (t % YS) * 2 + core)

    def greet(device):
        pl.semaphore_signal(barrier, inc=1, device_id=device, device_id_type=MESH)

    def each(count, fn):
        def step(d, carry):
            fn(d)
            return carry

        lax.fori_loop(1, count, step, 0, unroll=True)

    def gray(n):
        return n ^ (n >> 1)

    def far(d):
        i = d - 1
        mixed = (i >= 4) & (i < 12)
        xi = jnp.where(mixed, (i - 4) >> 1, i & 3)
        zz = jnp.where(mixed, 3 - 2 * (i & 1), jnp.where(i < 4, 2, 0))
        return q ^ (4 * gray(3 - xi) + zz)

    each(NCTX, lambda d: greet(at_ctx(far(d))))
    if full:
        each(TRIPLE, lambda d: greet(at_triple((me + d) % TRIPLE)))
        greet(at_group(m + 1 - 2 * core))
    for copy in copies[2:]:
        copy.start()
    ext2[...] = jnp.zeros_like(ext2)

    def remote(src, dst, ss, rs, device):
        return pltpu.make_async_remote_copy(
            src_ref=src, dst_ref=dst, send_sem=ss, recv_sem=rs,
            device_id=device, device_id_type=MESH,
        )

    copies[0].wait()
    rows = [field_ref[f, :, c, :] for f in range(2) for c in range(CHAN)]
    x = split(jnp.concatenate(rows, axis=0), 1, (0, 0, 1))
    y1 = dot(first_ref[...], x, ((1,), (1,))).reshape(NCTX, 2, SLOTS, RADIX)
    copies[1].wait()
    sub = lax.broadcasted_iota(jnp.int32, (SLOTS, HALF), 0)
    keep = (lax.broadcasted_iota(jnp.int32, (NCTX, SLOTS, HALF), 0)
            + lax.broadcasted_iota(jnp.int32, (NCTX, SLOTS, HALF), 1)) > 0
    tc = turn_ref[0, :HALF].reshape(NCTX, SLOTS, HALF)
    ts = turn_ref[1, :HALF].reshape(NCTX, SLOTS, HALF)
    ec, es = turn_ref[0, HALF:], turn_ref[1, HALF:]
    extra = jnp.zeros((SLOTS, HALF), F32)
    for f in range(2):
        lanes = slice(f * HALF, (f + 1) * HALF)
        re = y1[:, 0, :, lanes]
        im = y1[:, 1, :, lanes]
        mid = jnp.broadcast_to(im[0, 0:1, :], (SLOTS, HALF))
        extra = jnp.where(sub == 2 * f, mid * ec, extra)
        extra = jnp.where(sub == 2 * f + 1, -mid * es, extra)
        im = jnp.where(keep, im, 0.0)
        send1[:, 2 * f] = re * tc + im * ts
        send1[:, 2 * f + 1] = im * tc - re * ts
    send1[SPECIAL, 4] = extra
    recv1[q, 0:4] = send1[q, 0:4]

    @pl.when(q == SPECIAL)
    def _():
        recv1[SPECIAL, 4] = send1[SPECIAL, 4]

    pl.semaphore_wait(barrier, NCTX - 1 + (TRIPLE if full else 0))

    def tiles(special, count, act):
        @pl.when(special)
        def _():
            act(count + 1)

        @pl.when(jnp.logical_not(special))
        def _():
            act(count)

    def out1(p, count):
        return remote(
            send1.at[p, pl.ds(0, count)], recv1.at[q, pl.ds(0, count)], s1.at[p], r1.at[q], at_ctx(p))

    def in1(p, count):
        return remote(
            send1.at[p, pl.ds(0, count)], recv1.at[p, pl.ds(0, count)], s1.at[p], r1.at[p], at_ctx(p))

    def start1(d):
        p = far(d)
        tiles(p == SPECIAL, 4, lambda n: out1(p, n).start())

    each(NCTX, start1)
    for copy in copies[2:]:
        copy.wait()
    tiles(q == SPECIAL, 4, lambda n: each(NCTX, lambda d: in1(((q + d) & (NCTX - 1)), n).wait_recv()))

    def lane_ids(rows):
        return lax.broadcasted_iota(jnp.int32, (rows, HALF), 1)

    halves = [
        block_transpose([recv1[8 * h + j].reshape(40, HALF) for j in range(8)], lane_ids(40))
        for h in range(2)
    ]
    per_c = [jnp.concatenate([halves[0][c], halves[1][c]], axis=1) for c in range(CHAN)]
    for c in range(CHAN):
        ext[c] = per_c[c][32:40]
    planes = [per_c[c][8 * r : 8 * r + 8] for r in range(4) for c in range(CHAN)]
    planes += [ext[:, r, :] for r in range(4)]
    square = square_ref[...]
    spec = dot(split(jnp.concatenate(planes, axis=0), 1, (0, 1, 0)), square)

    def forward(r):
        out = []
        for base, size in ((64 * r, 64), (256 + 8 * r, 8)):
            re, im = spec[base : base + size], spec[base + size : base + 2 * size]
            out.append((re[:, :RADIX] + im[:, RADIX:], im[:, :RADIX] - re[:, RADIX:]))
        return out

    us, gs = forward(0), forward(2)
    bc, bs = back_ref[0, :8], back_ref[1, :8]
    xc, xs = back_ref[0, 8:], back_ref[1, 8:]

    def out2(f, p, count):
        return remote(
            send2.at[f, p, pl.ds(0, count)], recv2.at[f, q, pl.ds(0, count)],
            s2.at[f, p], r2.at[f, q], at_ctx(p))

    def in2(f, p, count):
        return remote(
            send2.at[f, p, pl.ds(0, count)], recv2.at[f, p, pl.ds(0, count)],
            s2.at[f, p], r2.at[f, p], at_ctx(p))

    def inverse(f, main, side):
        inv = dot(split(jnp.concatenate(main + side, axis=0), 1, (0, 1, 0)), square)
        re, im, xr, xi = inv[:64], inv[64:128], inv[128:136], inv[136:144]
        qr = (re[:, :RADIX] - im[:, RADIX:]).reshape(CHAN, SLOTS, RADIX)
        qi = (im[:, :RADIX] + re[:, RADIX:]).reshape(CHAN, SLOTS, RADIX)
        outs = (qr * bc[None] - qi * bs[None], qi * bc[None] + qr * bs[None])
        er = xr[:, :RADIX] - xi[:, RADIX:]
        ei = xi[:, :RADIX] + xr[:, RADIX:]
        ext2[f, :, 0, :] = er * xc - ei * xs
        per_c = [jnp.concatenate([outs[0][c], outs[1][c], ext2[f, c]], axis=0) for c in range(CHAN)]
        for h in range(2):
            parts = [v[:, h * HALF : (h + 1) * HALF] for v in per_c]
            for j, value in enumerate(block_transpose(parts, lane_ids(24))):
                send2[f, 8 * h + j] = value.reshape(3, SLOTS, HALF)
        recv2[f, q] = send2[f, q]

    def leave(f):
        tiles(q == SPECIAL, 2, lambda n: each(NCTX, lambda d: out2(f, far(d), n).start()))


    def collect(f):
        def arrive(d):
            p = ((q + d) & (NCTX - 1))
            tiles(p == SPECIAL, 2, lambda n: in2(f, p, n).wait_recv())

        each(NCTX, arrive)
        recv2[f, 0, 1, 0:1, :] = recv2[f, SPECIAL, 2, 0:1, :]
        values = split(recv2[f, :, 0:2].reshape(RADIX, HALF), 0, (0, 0, 1))
        return dot(last_ref[...], values).T

    corr = [
        [gr * ar + gi * ai, gi * ar - gr * ai]
        for (ar, ai), (gr, gi) in zip(us, gs)
    ]
    inverse(0, corr[0], corr[1])
    leave(0)
    low = q < NCTX // 2
    hr = jnp.where(low, h_ref[0, :, 0:8, :], h_ref[0, :, 1:9, :]).reshape(64, RADIX)
    hi = jnp.where(low, h_ref[1, :, 0:8, :], h_ref[1, :, 1:9, :]).reshape(64, RADIX)
    hs = [(hr, hi), (h_ref[0, :, 0, :], h_ref[1, :, 0, :])]
    prod = [
        [fr * gr + fi * gi, fr * gi - fi * gr]
        for (fr, fi), (gr, gi) in zip(hs, gs)
    ]
    inverse(1, prod[0], prod[1])

    part[...] = collect(0).reshape(CHAN, COLS, HALF)

    def near(d):
        return (y + jnp.where((d & 1) == 1, (d + 1) >> 1, YS - (d >> 1))) & (YS - 1)

    def out_rs(t):
        return remote(part.at[t % YS], gathered.at[me], rs_s.at[t], rs_r.at[me], at_triple(t))

    def in_rs(t):
        return remote(part.at[t % YS], gathered.at[t], rs_s.at[t], rs_r.at[t], at_triple(t))

    if full:
        for dz in (1, 2):
            other = (zl + dz) % ZS * YS
            each(YS, lambda d: out_rs(other + near(YS - d)).start())
            out_rs(other + y).start()
        each(YS, lambda d: out_rs(zl * YS + near(YS - d)).start())
        gathered[me] = part[y]

    leave(1)

    if full:
        each(TRIPLE, lambda d: in_rs((me + d) % TRIPLE).wait_recv())
        everyone[core, y] = jnp.sum(gathered[...], axis=0)
        twin = at_group(m + 1 - 2 * core)

        def out_ag(yy):
            return remote(
                everyone.at[core, y], everyone.at[core, y], ag_s.at[yy], ag_r.at[y], at_group(yy * 2 + core))

        def in_ag(yy):
            return remote(
                everyone.at[core, yy], everyone.at[core, yy], ag_s.at[yy], ag_r.at[yy], at_group(yy * 2 + core))

        def out_twin(yy):
            return remote(everyone.at[core, yy], everyone.at[core, yy], c_s.at[yy], c_r.at[yy], twin)

        def in_twin(yy):
            return remote(everyone.at[1 - core, yy], everyone.at[1 - core, yy], c_s.at[yy], c_r.at[yy], twin)

        def hand_on(d):
            in_ag(near(d)).wait_recv()
            out_twin(near(d)).start()

        each(YS, lambda d: out_ag(near(YS - d)).start())
        out_twin(y).start()
        own = collect(1)
        for c in range(CHAN):
            in_out[:, c, :] = own[COLS * c : COLS * (c + 1)]
        each(YS, hand_on)

        def place(which):
            @pl.when(which == 0)
            def _():
                for f in range(CHAN):
                    filt_out[:, f, :] = everyone[0, f]

            @pl.when(which == 1)
            def _():
                for f in range(CHAN):
                    filt_out[:, CHAN + f, :] = everyone[1, f]

        place(core)
        in_twin(y).wait_recv()
        each(YS, lambda d: in_twin(near(d)).wait_recv())
        place(1 - core)
        each(TRIPLE, lambda d: out_rs((me + d) % TRIPLE).wait_send())
        each(YS, lambda d: out_ag(((y + d) & (YS - 1))).wait_send())
        each(YS, lambda d: out_twin(((y + d) & (YS - 1))).wait_send())
        out_twin(y).wait_send()
    else:
        own = collect(1)
        for c in range(CHAN):
            in_out[:, c, :] = own[COLS * c : COLS * (c + 1)]
        for f in range(2 * CHAN):
            filt_out[:, f, :] = part[f % CHAN]

    def finish1(d):
        p = ((q + d) & (NCTX - 1))
        tiles(p == SPECIAL, 4, lambda n: out1(p, n).wait_send())

    each(NCTX, finish1)
    for f in range(2):
        tiles(q == SPECIAL, 2, lambda n: each(NCTX, lambda d: out2(f, ((q + d) & (NCTX - 1)), n).wait_send()))


def body(saved_input, out_grad, filter_spec):
    full = lax.axis_size("ch") > 1
    first, turn, square, back, last = (jnp.asarray(t) for t in tables())
    vm = pl.BlockSpec(memory_space=pltpu.VMEM)
    hbm = pl.BlockSpec(memory_space=pltpu.HBM)
    sem = pltpu.SemaphoreType.DMA
    v = pltpu.VMEM
    return pl.pallas_call(
        functools.partial(kernel, full),
        out_shape=(
            jax.ShapeDtypeStruct((COLS, CHAN, HALF), F32),
            jax.ShapeDtypeStruct((COLS, 2 * CHAN, HALF), F32),
        ),
        in_specs=[vm] + [hbm] * 6,
        out_specs=(vm, vm),
        scratch_shapes=[
            v((RADIX, 3 * HALF), BF16),
            v((3 * RADIX, 2 * RADIX), BF16),
            v((HALF, 3 * RADIX), BF16),
            v((2, CHAN, 16, RADIX), F32),
            v((2, HALF + 8, HALF), F32),
            v((2, 16, RADIX), F32),
            v((NCTX, 5, SLOTS, HALF), F32),
            v((NCTX, 5, SLOTS, HALF), F32),
            v((2, NCTX, 3, SLOTS, HALF), F32),
            v((2, NCTX, 3, SLOTS, HALF), F32),
            v((CHAN, 8, RADIX), F32),
            v((2, CHAN, 8, RADIX), F32),
            v((CHAN, COLS, HALF), F32),
            v((TRIPLE, COLS, HALF), F32),
            v((2, CHAN, COLS, HALF), F32),
            sem((6,)),
            sem((NCTX,)), sem((NCTX,)), sem((2, NCTX)), sem((2, NCTX)),
            sem((TRIPLE,)), sem((TRIPLE,)),
            sem((YS,)), sem((YS,)), sem((YS,)), sem((YS,)),
        ],
        compiler_params=pltpu.CompilerParams(
            collective_id=0, has_side_effects=True, vmem_limit_bytes=56_229_888
        ),
        cost_estimate=pl.CostEstimate(flops=400_000_000, bytes_accessed=2_000_000, transcendentals=0),
    )(jnp.stack([saved_input, out_grad]), filter_spec, first, turn, square, back, last)


def solution(mesh):
    placed = (P("ctx", "ch", None), P("ctx", "ch", None), P(None, None, "ctx", None))
    return jax.shard_map(
        body,
        mesh=mesh,
        in_specs=placed,
        out_specs=(P("ctx", "ch", None), P("ctx", None, None)),
        check_vma=False,
    )
```
